128 devices in a mesh: ctx: 128 (over y, z, x, core).
Axes of the slice: x: 4, y: 4, z: 4, core: 2. Of those that a mesh axis runs over, the one named last changes fastest.
Arguments:
- context_q: bfloat16 [32768, 8192], P('ctx'), may hold values from -12 to 12
- context_k: bfloat16 [32768, 1024], P('ctx'), may hold values from -6 to 6
- context_v: bfloat16 [32768, 1024], P('ctx'), may hold values from -6 to 6
- question: bfloat16 [128, 8192], P('ctx')
- valid: int32 [128], replicated, may hold values from 1 to 256, 24576 in all
- qlen: int32 [1], replicated, may hold values from 64 to 128
Outputs:
- encoded: bfloat16 [32768, 8192], P('ctx')
- answer: bfloat16 [128, 8192], P('ctx')
The draws below stay inside these ranges and needn't reach their ends.
All inputs are finite; a program needn't handle non-finite values.
Results may differ from the reference program's by a relative error of at most 0.006.
Values may be sent and summed in bfloat16 or wider, within the bound.
A program may use at most 128 MiB of HBM per device.

```python
import math
import jax
import jax.numpy as jnp
import numpy as np
from jax import lax

H = 64
KVH = 8
DH = 128
BLK = 256
QL = 128
N_CTX = 128


def draw_question(key, part):
    key = jax.random.fold_in(key, 11)
    noise_key, scale_key = jax.random.split(key)
    values = jax.random.normal(noise_key, (QL, H * DH), jnp.float32)
    row_scale = 3.0 + 0.0 * jax.random.uniform(scale_key, (QL, 1), jnp.float32)
    return (values * row_scale).astype(jnp.bfloat16)


def shard_levels(stream_key, shape, cuts, low, largest):
    gain, own = 1.0, jax.random.fold_in(stream_key, 6)
    for axis_at, shards_of in cuts:
        draws = jnp.exp(jax.random.uniform(jax.random.fold_in(own, axis_at), (shards_of,), jnp.float32, low / len(cuts), largest / len(cuts)))
        gain = gain * jnp.repeat(draws, shape[axis_at] // shards_of).reshape([-1 if axis == axis_at else 1 for axis in range(len(shape))])
    return gain


def profile(count, total, bound, lean):
    portions = [(1 << 20) // math.isqrt(standing ** lean) + 1 for standing in range(2, count + 1)]
    rest, holding = total - bound - (count - 1), [1] * (count - 1)
    while rest > 0:
        free = [i for i in range(count - 1) if holding[i] < bound]
        mass, left = sum([portions[i] for i in free]), rest
        for i in free:
            addition = min(bound - holding[i], max(1, left * portions[i] // mass), rest)
            holding[i] = holding[i] + addition
            rest = rest - addition
    return np.array([bound] + holding)


def ragged(own_key, count, total, bound, lean):
    if count == 2:
        one = jax.random.randint(own_key, (), max(1, total - bound), min(bound, total - 1) + 1)
        return jnp.stack([one, total - one])
    sizes = jnp.asarray(profile(count, total, bound, lean), jnp.int32)
    twos = (count - 1) // 2
    giver, sink = sizes[1:1 + 2 * twos:2], sizes[2:2 + 2 * twos:2]
    room = jnp.minimum(giver - 1, bound - sink)
    shifted = jax.random.randint(jax.random.fold_in(own_key, 1), (twos,), 0, 1 << 20) % (room + 1)
    sizes = sizes.at[1:1 + 2 * twos:2].set(giver - shifted).at[2:2 + 2 * twos:2].set(sink + shifted)
    return sizes[jax.random.permutation(jax.random.fold_in(own_key, 2), count)]


def bell_draw(key, dims, scale, limit, cuts=(), kind=jnp.bfloat16):
    array = scale * jax.random.normal(key, dims, jnp.float32)
    if cuts:
        array = array * shard_levels(key, dims, cuts, -0.22, 0.18)
    return jnp.clip(array, -limit, limit).astype(kind)


def setup_inputs(seed: int = 0) -> dict:
    seeds = jax.random.split(jax.random.key(seed), 7)
    return {
        "context_q": bell_draw(seeds[0], (BLK * N_CTX, H * DH), 2.0, 12.0, ((0, 128),)),
        "context_k": bell_draw(seeds[1], (BLK * N_CTX, KVH * DH), 1.0, 6.0, ((0, 128),)),
        "context_v": bell_draw(seeds[2], (BLK * N_CTX, KVH * DH), 1.0, 6.0, ((0, 128),)),
        "question": draw_question(jax.random.fold_in(seeds[6], 71), 0),
        "valid": ragged(seeds[4], N_CTX, N_CTX * BLK * 3 // 4, BLK, 0).astype(jnp.int32),
        "qlen": jax.random.randint(seeds[5], (1,), QL // 2, QL + 1).astype(jnp.int32),
    }


neg_fill = -1e30


def attend(queries, keys_all, values_all, allowed):
    query_count = queries.shape[0]
    per_group = H // KVH
    outputs, maxima, totals = [], [], []
    for group_index in range(KVH):
        low = group_index * per_group * DH
        q_group = queries[:, low:low + per_group * DH].reshape(query_count, per_group, DH).astype(jnp.float32)
        k_group = keys_all[:, group_index * DH:(group_index + 1) * DH].astype(jnp.float32)
        v_group = values_all[:, group_index * DH:(group_index + 1) * DH].astype(jnp.float32)
        scores = jnp.einsum("rhd,kd->hrk", q_group, k_group) * (DH ** -0.5)
        scores = jnp.where(allowed[None], scores, neg_fill)
        row_peak = jnp.max(scores, axis=2, keepdims=True)
        weights = jnp.exp(scores - row_peak)
        totals.append(jnp.sum(weights, axis=2).T)
        maxima.append(row_peak[:, :, 0].T)
        rounded = lax.optimization_barrier(weights.astype(jnp.bfloat16)).astype(jnp.float32)
        mixed_out = jnp.einsum("hrk,kd->rhd", rounded, v_group)
        outputs.append(mixed_out.reshape(query_count, per_group * DH))
    return jnp.concatenate(outputs, 1), jnp.concatenate(maxima, 1), jnp.concatenate(totals, 1)


def encode(block_q, block_k, block_v, anchor_k, anchor_v, valid_here, valid_first, position):
    block_size = block_q.shape[0]
    query_index = jnp.arange(block_size)[:, None]
    key_index = jnp.arange(2 * block_size)[None, :]
    anchor_ok = (key_index < block_size) & (key_index < valid_first) & (position > 0)
    local_index = key_index - block_size
    local_ok = (key_index >= block_size) & (local_index <= query_index) & (local_index < valid_here)
    keys_all = jnp.concatenate([anchor_k, block_k], 0)
    values_all = jnp.concatenate([anchor_v, block_v], 0)
    output, maxima, totals = attend(block_q, keys_all, values_all, anchor_ok | local_ok)
    normed = output / jnp.repeat(totals, DH, axis=1)
    live_rows = jnp.arange(block_size)[:, None] < valid_here
    return jnp.where(live_rows, normed, 0.0).astype(jnp.bfloat16)


def reference(context_q, context_k, context_v, question, valid, qlen):
    blocks_q = context_q.reshape(N_CTX, BLK, H * DH)
    blocks_k = context_k.reshape(N_CTX, BLK, KVH * DH)
    blocks_v = context_v.reshape(N_CTX, BLK, KVH * DH)
    anchor_k = blocks_k[0]
    anchor_v = blocks_v[0]
    valid_first = valid[0]

    def encode_block(pieces):
        piece_q, piece_k, piece_v, valid_here, position = pieces
        return encode(piece_q, piece_k, piece_v, anchor_k, anchor_v, valid_here, valid_first, position)

    encoded = lax.map(encode_block, (blocks_q, blocks_k, blocks_v, valid, jnp.arange(N_CTX, dtype=jnp.int32)))
    encoded = encoded.reshape(N_CTX * BLK, H * DH)

    def absorb(state_now, pieces):
        global_top, numerator, denominator = state_now
        piece_k, piece_v, valid_here = pieces
        allowed = jnp.broadcast_to(jnp.arange(BLK)[None, :] < valid_here, (QL, BLK))
        partial_out, local_peak, local_sum = attend(question, piece_k, piece_v, allowed)
        new_top = jnp.maximum(global_top, local_peak)
        old_scale = jnp.exp(global_top - new_top)
        new_scale = jnp.exp(local_peak - new_top)
        numerator = numerator * jnp.repeat(old_scale, DH, axis=1) + partial_out * jnp.repeat(new_scale, DH, axis=1)
        denominator = denominator * old_scale + local_sum * new_scale
        return (new_top, numerator, denominator), None

    start_state = (jnp.full((QL, H), neg_fill, jnp.float32), jnp.zeros((QL, H * DH), jnp.float32), jnp.zeros((QL, H), jnp.float32))
    final_state, unused = lax.scan(absorb, start_state, (blocks_k, blocks_v, valid))
    numerator, denominator = final_state[1], final_state[2]
    live_rows = (jnp.arange(QL) < qlen[0])[:, None]
    answer = jnp.where(live_rows, numerator / jnp.repeat(denominator, DH, axis=1), 0.0).astype(jnp.bfloat16)
    return encoded, answer
```

```python
import functools

import jax
import jax.numpy as jnp
from jax import lax
from jax.experimental import pallas as pl
from jax.experimental.pallas import tpu as pltpu
from jax.sharding import PartitionSpec as P

H = 64
KVH = 8
DH = 128
BLK = 256
N = 128
GROUP = H // KVH
EXP2_SCALE = 1.4426950408889634 * DH ** (-0.5)

f32 = jnp.float32
bf16 = jnp.bfloat16
MESH = pl.DeviceIdType.MESH
NT = (((1,), (1,)), ((), ()))


def stride_of(axis):
    return 2 + 6 * axis + 9 * axis * (axis - 1)


def send(src, dst, send_sem, recv_sem, device):
    pltpu.make_async_remote_copy(
        src_ref=src, dst_ref=dst, send_sem=send_sem, recv_sem=recv_sem,
        device_id=(device,), device_id_type=MESH,
    ).start()


def drain(ref, sem):
    pltpu.make_async_copy(ref, ref, sem).wait()


def comm_kernel(
    question_ref, k_ref, v_ref, valid_ref, qlen_ref,
    answer_ref, anchor_out,
    q64, kvs, kvbuf, ones, rows_in, q_all, part_out, lse_out, part_in, lse_in, fin_out, fin_in, anchor,
    s_rows, r_rows, s_q, r_q, s_kv, r_kv, s_anc, r_anc, s_part, r_part, s_lse, r_lse, s_fin, r_fin, own_sem,
):
    me = lax.axis_index("ctx")
    core = me % 2
    x = (me // 2) % 4
    z = (me // 8) % 4
    y = me // 32
    cls = (x + y + z) % 4
    head = 2 * cls + core
    line = me // 8
    member = me % 8

    barrier = pltpu.get_barrier_semaphore()

    def greet(i, carry):
        pl.semaphore_signal(barrier, inc=1, device_id=((me + 1 + i) % N,), device_id_type=MESH)
        return carry

    lax.fori_loop(0, N - 1, greet, 0)

    valid_here = valid_ref[me]
    live = lax.broadcasted_iota(jnp.int32, (BLK, DH), 0) < valid_here
    for h in range(KVH):
        cols = slice(h * DH, (h + 1) * DH)
        k_h = k_ref[:, cols].astype(f32)
        v_h = v_ref[:, cols].astype(f32)
        kvs[h * 512:h * 512 + 256, :] = jnp.where(live, k_h, k_h[0:1, :]).astype(bf16)
        kvs[h * 512 + 256:h * 512 + 512, :] = jnp.where(live, v_h, 0.0).astype(bf16)
    for h in range(H):
        q64[h:h + 1, :] = question_ref[:, h * DH:(h + 1) * DH].astype(f32)
    axis = head % 3
    stride = stride_of(axis)
    first = me - core - ((me // stride) % 4) * stride
    for b in range(8):
        valid_b = valid_ref[first + (b // 2) * stride + b % 2]
        ones[b * BLK:(b + 1) * BLK, :] = jnp.where(
            lax.broadcasted_iota(jnp.int32, (BLK, DH), 0) < valid_b, 1.0, 0.0).astype(bf16)

    pl.semaphore_wait(barrier, N - 1)

    def send_rows(d, carry):
        other = (head + d) % 8
        target = me - member + ((other // 2 + 8 - y - z) % 4) * 2 + other % 2
        send(q64.at[pl.ds(other * 8, 8)], rows_in.at[member], s_rows, r_rows, target)
        return carry

    lax.fori_loop(1, 8, send_rows, 0)
    rows_in[member] = q64[pl.ds(head * 8, 8), :]

    def send_kv(d, carry):
        other = (head + d) % 8
        step = stride_of(other % 3)
        at = (me // step) % 4
        target = me - core + ((at + other // 2 + 4 - cls) % 4 - at) * step + other % 2
        send(kvs.at[pl.ds(other * 512, 512)], kvbuf.at[pl.ds((at * 2 + core) * 512, 512)], s_kv, r_kv, target)
        return carry

    at_home = (me // stride) % 4
    own_kv = pltpu.make_async_copy(
        kvs.at[pl.ds(head * 512, 512)], kvbuf.at[pl.ds((at_home * 2 + core) * 512, 512)], own_sem)
    own_kv.start()

    @pl.when(me == 0)
    def _():
        def scatter(j, carry):
            send(kvs.at[pl.ds(32 * j, 32)], anchor.at[pl.ds(32 * j, 32)], s_anc.at[0], r_anc.at[0], 2 * j)
            return carry

        def scatter_odd(j, carry):
            piece = 2048 + 32 * (((j // 4) % 4) * 16 + (j % 4) * 4 + j // 16)
            send(kvs.at[pl.ds(piece, 32)], anchor.at[pl.ds(piece, 32)], s_anc.at[5], r_anc.at[0], 2 * j + 1)
            return carry

        lax.fori_loop(0, 64, scatter_odd, 0)
        lax.fori_loop(1, 64, scatter, 0)
        anchor[0:32, :] = kvs[0:32, :]

    lax.fori_loop(1, 8, send_kv, 0)

    drain(rows_in.at[pl.ds(0, 7)], r_rows)
    q_all[pl.ds(line * 64, 64), :] = rows_in[...].reshape(64, DH).astype(bf16)

    def peer(d):
        other = (line + d) % 16
        return other, (other * 4 + (cls + 8 - other // 4 - other % 4) % 4) * 2 + core

    def send_q(d, carry):
        other, target = peer(d)
        send(q_all.at[pl.ds(line * 64, 64)], q_all.at[pl.ds(line * 64, 64)], s_q, r_q, target)
        return carry

    lax.fori_loop(1, 16, send_q, 0)

    st = (2 + 30 * core, 8 - 6 * core, 32 - 24 * core)
    at = [(me // s) % 4 for s in st]
    half = 2048 * core
    starts = (half + 32 * (at[2] * 16 + at[1] * 4 + at[0]), half + 32 * (at[2] * 16 + at[1] * 4), half + 32 * at[2] * 16)
    sizes = (32, 128, 512)

    def gather_stage(n):
        piece = anchor.at[pl.ds(starts[n], sizes[n])]
        for d in (1, 2, 3):
            target = me + ((at[n] + d) % 4 - at[n]) * st[n]
            send(piece, piece, s_anc.at[n + 1], r_anc.at[n + 1], target)

    def gather_wait(n):
        drain(anchor.at[pl.ds(0, 3 * sizes[n])], r_anc.at[n + 1])

    @pl.when(me != 0)
    def _():
        drain(anchor.at[pl.ds(0, 32)], r_anc.at[0])

    gather_stage(0)
    gather_wait(0)
    gather_stage(1)

    drain(q_all.at[pl.ds(0, 15 * 64)], r_q)
    own_kv.wait()
    drain(kvbuf.at[pl.ds(0, 7 * 512)], r_kv)
    gather_wait(1)
    gather_stage(2)

    diag = lax.broadcasted_iota(jnp.int32, (64, DH), 0) == lax.broadcasted_iota(jnp.int32, (64, DH), 1)

    def attend(i, carry):
        rows = pl.ds(pl.multiple_of(i * 128, 128), 128)
        q = q_all[rows, :]
        s = [lax.dot_general(q, kvbuf[b * 512:b * 512 + 256, :], NT, preferred_element_type=f32) for b in range(8)]
        peak = functools.reduce(jnp.maximum, [jnp.max(s_b, axis=1, keepdims=True) for s_b in s]) * EXP2_SCALE
        p = jnp.concatenate([jnp.exp2(s_b * EXP2_SCALE - peak).astype(bf16) for s_b in s], axis=1)
        v = jnp.concatenate(
            [jnp.concatenate([kvbuf[b * 512 + 256:b * 512 + 512, :], ones[b * BLK:(b + 1) * BLK, :]], axis=1) for b in range(8)], axis=0)
        o = jnp.dot(p, v, preferred_element_type=f32)
        total = o[:, DH:]
        part_out[rows, :] = (o[:, :DH] / total).astype(bf16)
        lse = peak + jnp.log2(total)
        for n in range(2):
            flat = jnp.sum(jnp.where(diag, lse[n * 64:(n + 1) * 64], 0.0), axis=0, keepdims=True)
            lse_out[2 * i + n] = jnp.broadcast_to(flat, (8, DH))
        return carry

    lax.fori_loop(0, 8, attend, 0)

    def send_part(d, carry):
        other, target = peer(d)
        send(part_out.at[pl.ds(other * 64, 64)], part_in.at[pl.ds(line * 64, 64)], s_part, r_part, target)
        send(lse_out.at[other], lse_in.at[line], s_lse, r_lse, target)
        return carry

    lax.fori_loop(1, 16, send_part, 0)
    part_in[pl.ds(line * 64, 64), :] = part_out[pl.ds(line * 64, 64), :]
    lse_in[line] = lse_out[line]

    gather_wait(2)
    mine = anchor.at[pl.ds(half, 2048)]
    send(mine, mine, s_anc.at[4], r_anc.at[4], me + 1 - 2 * core)

    drain(part_in.at[pl.ds(0, 15 * 64)], r_part)
    drain(lse_in.at[pl.ds(0, 15)], r_lse)
    lse_all = lse_in[...]
    weight = jnp.exp2(lse_all - jnp.max(lse_all, axis=0, keepdims=True))
    weight = weight / jnp.sum(weight, axis=0, keepdims=True)
    merged = jnp.zeros((64, DH), f32)
    for j in range(16):
        column = jnp.sum(jnp.where(diag, weight[j, 0:1, :], 0.0), axis=1, keepdims=True)
        merged += column * part_in[j * 64:(j + 1) * 64, :].astype(f32)
    fin_out[...] = merged.reshape(8, 8, DH)

    def send_fin(d, carry):
        other = (member + d) % 8
        send(fin_out.at[other], fin_in.at[head], s_fin, r_fin, me - member + other)
        return carry

    lax.fori_loop(1, 8, send_fin, 0)
    fin_in[head] = fin_out[member]
    drain(fin_in.at[pl.ds(0, 7)], r_fin)
    answer_ref[...] = jnp.where(me < qlen_ref[0], fin_in[...].reshape(64, DH), 0.0)

    drain(anchor.at[pl.ds(0, 2048)], r_anc.at[4])
    anchor_out[...] = anchor[...]

    drain(rows_in.at[pl.ds(0, 7)], s_rows)
    drain(kvbuf.at[pl.ds(0, 7 * 512)], s_kv)
    drain(q_all.at[pl.ds(0, 15 * 64)], s_q)
    drain(part_in.at[pl.ds(0, 15 * 64)], s_part)
    drain(lse_in.at[pl.ds(0, 15)], s_lse)
    drain(fin_in.at[pl.ds(0, 7)], s_fin)
    for n in range(3):
        drain(anchor.at[pl.ds(0, 3 * sizes[n])], s_anc.at[n + 1])
    drain(anchor.at[pl.ds(0, 2048)], s_anc.at[4])

    @pl.when(me == 0)
    def _():
        drain(anchor.at[pl.ds(0, 63 * 32)], s_anc.at[0])
        drain(anchor.at[pl.ds(0, 2048)], s_anc.at[5])


def exchange(question, k, v, valid, qlen):
    vmem = pl.BlockSpec(memory_space=pltpu.VMEM)
    smem = pl.BlockSpec(memory_space=pltpu.SMEM)
    dma = pltpu.SemaphoreType.DMA
    return pl.pallas_call(
        comm_kernel,
        out_shape=(jax.ShapeDtypeStruct((H, DH), f32), jax.ShapeDtypeStruct((KVH * 512, DH), bf16)),
        in_specs=[vmem, vmem, vmem, smem, smem],
        out_specs=(vmem, vmem),
        scratch_shapes=[
            pltpu.VMEM((H, DH), f32),
            pltpu.VMEM((KVH * 512, DH), bf16),
            pltpu.VMEM((8 * 512, DH), bf16),
            pltpu.VMEM((8 * BLK, DH), bf16),
            pltpu.VMEM((8, 8, DH), f32),
            pltpu.VMEM((16 * 64, DH), bf16),
            pltpu.VMEM((16 * 64, DH), bf16),
            pltpu.VMEM((16, 8, DH), f32),
            pltpu.VMEM((16 * 64, DH), bf16),
            pltpu.VMEM((16, 8, DH), f32),
            pltpu.VMEM((8, 8, DH), f32),
            pltpu.VMEM((8, 8, DH), f32),
            pltpu.VMEM((KVH * 512, DH), bf16),
            dma, dma, dma, dma, dma, dma, dma((6,)), dma((5,)), dma, dma, dma, dma, dma, dma, dma,
        ],
        compiler_params=pltpu.CompilerParams(collective_id=0, has_side_effects=True, vmem_limit_bytes=40 << 20),
        name="exchange",
    )(question, k, v, valid, qlen)


def encode_kernel(valid_ref, where_ref, q_ref, k_ref, v_ref, anchor_ref, out_ref):
    position = where_ref[0]
    valid_here = valid_ref[position]
    valid_first = jnp.where(position > 0, valid_ref[0], 0)
    row = lax.broadcasted_iota(jnp.int32, (BLK, DH), 0)
    live = row < valid_here
    anchored = row < valid_first
    k_own = k_ref[...].astype(f32)
    k_own = jnp.where(live, k_own, k_own[0:1, :])
    k_first = anchor_ref[:BLK, :].astype(f32)
    k_first = jnp.where(position > 0, k_first, k_own[0:1, :])
    keys = jnp.concatenate([k_first.astype(bf16), k_own.astype(bf16)], axis=0)
    v_own = jnp.where(live, v_ref[...].astype(f32), 0.0).astype(bf16)
    v_first = jnp.where(anchored, anchor_ref[BLK:, :].astype(f32), 0.0).astype(bf16)
    values = jnp.concatenate([
        jnp.concatenate([v_first, jnp.where(anchored, 1.0, 0.0).astype(bf16)], axis=1),
        jnp.concatenate([v_own, jnp.where(live, 1.0, 0.0).astype(bf16)], axis=1),
    ], axis=0)
    causal = lax.broadcasted_iota(jnp.int32, (BLK, BLK), 1) <= lax.broadcasted_iota(jnp.int32, (BLK, BLK), 0)
    for h in range(GROUP):
        cols = slice(h * DH, (h + 1) * DH)
        s = lax.dot_general(q_ref[:, cols], keys, NT, preferred_element_type=f32)
        s_first = s[:, :BLK]
        s_own = jnp.where(causal, s[:, BLK:], -1e30)
        peak = jnp.maximum(jnp.max(s_first, axis=1, keepdims=True), jnp.max(s_own, axis=1, keepdims=True)) * EXP2_SCALE
        p = jnp.concatenate([jnp.exp2(s_first * EXP2_SCALE - peak), jnp.exp2(s_own * EXP2_SCALE - peak)], axis=1).astype(bf16)
        o = jnp.dot(p, values, preferred_element_type=f32)
        out_ref[:, cols] = jnp.where(live, o[:, :DH] / o[:, DH:], 0.0).astype(bf16)


def encode(q, k, v, anchor, valid, position):
    smem = pl.BlockSpec(memory_space=pltpu.SMEM)
    return pl.pallas_call(
        encode_kernel,
        grid=(KVH,),
        out_shape=jax.ShapeDtypeStruct((BLK, H * DH), bf16),
        in_specs=[
            smem, smem,
            pl.BlockSpec((BLK, GROUP * DH), lambda i: (0, i)),
            pl.BlockSpec((BLK, DH), lambda i: (0, i)),
            pl.BlockSpec((BLK, DH), lambda i: (0, i)),
            pl.BlockSpec((512, DH), lambda i: (i, 0)),
        ],
        out_specs=pl.BlockSpec((BLK, GROUP * DH), lambda i: (0, i)),
        compiler_params=pltpu.CompilerParams(vmem_limit_bytes=40 << 20),
        name="encode",
    )(valid, position, q, k, v, anchor)


def body(context_q, context_k, context_v, question, valid, qlen):
    answer, anchor = exchange(question, context_k, context_v, valid, qlen)
    position = lax.axis_index("ctx").reshape(1)
    encoded = encode(context_q, context_k, context_v, anchor, valid, position)
    return encoded, answer.reshape(1, H * DH).astype(bf16)


def solution(mesh):
    in_specs = (P("ctx", None), P("ctx", None), P("ctx", None), P("ctx", None), P(), P())
    out_specs = (P("ctx", None), P("ctx", None))
    return jax.shard_map(body, mesh=mesh, in_specs=in_specs, out_specs=out_specs, check_vma=False)
```

```python
import functools

import jax
import jax.numpy as jnp
from jax import lax
from jax.experimental import pallas as pl
from jax.experimental.pallas import tpu as pltpu
from jax.sharding import PartitionSpec as P

H = 64
KVH = 8
DH = 128
BLK = 256
N = 128
GROUP = H // KVH
EXP2_SCALE = 1.4426950408889634 * DH ** (-0.5)

f32 = jnp.float32
bf16 = jnp.bfloat16
MESH = pl.DeviceIdType.MESH
NT = (((1,), (1,)), ((), ()))

ROWS_AT = 2
GATHER_1_AT = 1
GATHER_2_AT = 5
MERGE_AT = 6


def stride_of(axis):
    return 2 + 6 * axis + 9 * axis * (axis - 1)


def send(src, dst, send_sem, recv_sem, device):
    pltpu.make_async_remote_copy(
        src_ref=src, dst_ref=dst, send_sem=send_sem, recv_sem=recv_sem,
        device_id=(device,), device_id_type=MESH,
    ).start()


def drain(ref, sem):
    pltpu.make_async_copy(ref, ref, sem).wait()


def star_kernel(
    q_hbm, k_hbm, v_hbm, question_hbm, valid_hbm, qlen_ref,
    out_ref, answer_ref,
    q_ref, k_ref, v_ref, question_ref, valid_ref,
    own_out, own_lse, q64, kvs, kvbuf, ones, rows_in, q_all, part_out, lse_out, part_in, lse_in, fin_out, fin_in, anchor,
    load_sem, s_rows, r_rows, s_q, r_q, s_kv, r_kv, s_anc, r_anc, s_part, r_part, s_lse, r_lse, s_fin, r_fin, own_sem,
):
    me = lax.axis_index("ctx")
    core = me % 2
    x = (me // 2) % 4
    z = (me // 8) % 4
    y = me // 32
    cls = (x + y + z) % 4
    head = 2 * cls + core
    line = me // 8
    member = me % 8

    loads = [
        pltpu.make_async_copy(src, dst, load_sem.at[n])
        for n, (src, dst) in enumerate([
            (valid_hbm, valid_ref), (k_hbm, k_ref), (v_hbm, v_ref), (question_hbm, question_ref),
            (q_hbm, q_ref)])
    ]
    for load in loads:
        load.start()

    barrier = pltpu.get_barrier_semaphore()

    def greet(i, carry):
        pl.semaphore_signal(barrier, inc=1, device_id=((me + 1 + i) % N,), device_id_type=MESH)
        return carry

    lax.fori_loop(0, N - 1, greet, 0)

    for load in loads[:4]:
        load.wait()
    valid_here = valid_ref[me]
    row = lax.broadcasted_iota(jnp.int32, (BLK, DH), 0)
    live = row < valid_here
    for h in range(H):
        q64[h:h + 1, :] = question_ref[:, h * DH:(h + 1) * DH].astype(f32)
    for h in range(KVH):
        cols = slice(h * DH, (h + 1) * DH)
        k_h = k_ref[:, cols].astype(f32)
        v_h = v_ref[:, cols].astype(f32)
        kvs[h * 512:h * 512 + 256, :] = jnp.where(live, k_h, k_h[0:1, :]).astype(bf16)
        kvs[h * 512 + 256:h * 512 + 512, :] = jnp.where(live, v_h, 0.0).astype(bf16)
    axis = head % 3
    stride = stride_of(axis)
    first = me - core - ((me // stride) % 4) * stride

    pl.semaphore_wait(barrier, N - 1)

    def send_rows(d, carry):
        other = (head + d) % 8
        target = me - member + ((other // 2 + 8 - y - z) % 4) * 2 + other % 2
        send(q64.at[pl.ds(other * 8, 8)], rows_in.at[member], s_rows, r_rows, target)
        return carry

    lax.fori_loop(1, 8, send_rows, 0)

    @pl.when(me == 0)
    def _():
        def scatter(j, carry):
            send(kvs.at[pl.ds(32 * j, 32)], anchor.at[pl.ds(32 * j, 32)], s_anc.at[0], r_anc.at[0], 2 * j)
            return carry

        def scatter_odd(j, carry):
            piece = 2048 + 32 * (((j // 4) % 4) * 16 + (j % 4) * 4 + j // 16)
            send(kvs.at[pl.ds(piece, 32)], anchor.at[pl.ds(piece, 32)], s_anc.at[5], r_anc.at[0], 2 * j + 1)
            return carry

        lax.fori_loop(0, 64, scatter_odd, 0)
        lax.fori_loop(1, 64, scatter, 0)
        anchor[0:32, :] = kvs[0:32, :]

    def send_kv(d, carry):
        other = (head + d) % 8
        step = stride_of(other % 3)
        at = (me // step) % 4
        target = me - core + ((at + other // 2 + 4 - cls) % 4 - at) * step + other % 2
        send(kvs.at[pl.ds(other * 512, 512)], kvbuf.at[pl.ds((at * 2 + core) * 512, 512)], s_kv, r_kv, target)
        return carry

    at_home = (me // stride) % 4
    own_kv = pltpu.make_async_copy(
        kvs.at[pl.ds(head * 512, 512)], kvbuf.at[pl.ds((at_home * 2 + core) * 512, 512)], own_sem)
    own_kv.start()
    lax.fori_loop(1, 8, send_kv, 0)
    rows_in[member] = q64[pl.ds(head * 8, 8), :]
    for b in range(8):
        valid_b = valid_ref[first + (b // 2) * stride + b % 2]
        ones[b * BLK:(b + 1) * BLK, :] = jnp.where(row < valid_b, 1.0, 0.0).astype(bf16)

    def peer(d):
        other = (line + d) % 16
        return other, peer_device(other)

    def peer_device(other):
        return (other * 4 + (cls + 8 - other // 4 - other % 4) % 4) * 2 + core

    st = (2 + 30 * core, 8 - 6 * core, 32 - 24 * core)
    at = [(me // s) % 4 for s in st]
    half = 2048 * core
    starts = (half + 32 * (at[2] * 16 + at[1] * 4 + at[0]), half + 32 * (at[2] * 16 + at[1] * 4), half + 32 * at[2] * 16)
    sizes = (32, 128, 512)

    def gather_stage(n):
        piece = anchor.at[pl.ds(starts[n], sizes[n])]
        for d in (1, 2, 3):
            target = me + ((at[n] + d) % 4 - at[n]) * st[n]
            send(piece, piece, s_anc.at[n + 1], r_anc.at[n + 1], target)

    def gather_wait(n):
        drain(anchor.at[pl.ds(0, 3 * sizes[n])], r_anc.at[n + 1])

    loads[4].wait()
    causal = lax.broadcasted_iota(jnp.int32, (BLK, BLK), 1) <= lax.broadcasted_iota(jnp.int32, (BLK, BLK), 0)
    ones_own = jnp.where(live, 1.0, 0.0).astype(bf16)

    def own_block(g, carry):
        @pl.when(g == ROWS_AT)
        def _():
            drain(rows_in.at[pl.ds(0, 7)], r_rows)
            q_all[pl.ds(line * 64, 64), :] = rows_in[...].reshape(64, DH).astype(bf16)

            def send_q(d, carry):
                other, target = peer(d)
                send(q_all.at[pl.ds(line * 64, 64)], q_all.at[pl.ds(line * 64, 64)], s_q, r_q, target)
                return carry

            lax.fori_loop(1, 16, send_q, 0)

        base = pl.multiple_of(g * 512, 512)
        keys = kvs[pl.ds(base, 256), :]
        values = jnp.concatenate([kvs[pl.ds(base + 256, 256), :], ones_own], axis=1)
        for h in range(GROUP):
            cols = pl.ds(pl.multiple_of(g * GROUP * DH, GROUP * DH) + h * DH, DH)
            s = lax.dot_general(q_ref[:, cols], keys, NT, preferred_element_type=f32)
            s = jnp.where(causal, s, -1e30)
            peak = jnp.max(s, axis=1, keepdims=True) * EXP2_SCALE
            p = jnp.exp2(s * EXP2_SCALE - peak).astype(bf16)
            o = jnp.dot(p, values, preferred_element_type=f32)
            own_out[:, cols] = o[:, :DH] / o[:, DH:]
            own_lse[:, cols] = peak + jnp.log2(o[:, DH:])
        return carry

    lax.fori_loop(0, KVH, own_block, 0)

    @pl.when(me != 0)
    def _():
        drain(anchor.at[pl.ds(0, 32)], r_anc.at[0])

    gather_stage(0)

    drain(q_all.at[pl.ds(0, 15 * 64)], r_q)
    own_kv.wait()
    drain(kvbuf.at[pl.ds(0, 7 * 512)], r_kv)

    diag = lax.broadcasted_iota(jnp.int32, (64, DH), 0) == lax.broadcasted_iota(jnp.int32, (64, DH), 1)

    def attend(i, carry):
        @pl.when(i == GATHER_1_AT)
        def _():
            gather_wait(0)
            gather_stage(1)

        @pl.when(i == GATHER_2_AT)
        def _():
            gather_wait(1)
            gather_stage(2)

        chunk = (i + line // 2) % 8
        rows = pl.ds(pl.multiple_of(chunk * 128, 128), 128)
        q = q_all[rows, :]
        s = [lax.dot_general(q, kvbuf[b * 512:b * 512 + 256, :], NT, preferred_element_type=f32) for b in range(8)]
        peak = functools.reduce(jnp.maximum, [jnp.max(s_b, axis=1, keepdims=True) for s_b in s]) * EXP2_SCALE
        p = jnp.concatenate([jnp.exp2(s_b * EXP2_SCALE - peak).astype(bf16) for s_b in s], axis=1)
        v = jnp.concatenate(
            [jnp.concatenate([kvbuf[b * 512 + 256:b * 512 + 512, :], ones[b * BLK:(b + 1) * BLK, :]], axis=1) for b in range(8)], axis=0)
        o = jnp.dot(p, v, preferred_element_type=f32)
        total = o[:, DH:]
        part_out[rows, :] = (o[:, :DH] / total).astype(bf16)
        lse = peak + jnp.log2(total)
        for n in range(2):
            other = 2 * chunk + n
            flat = jnp.sum(jnp.where(diag, lse[n * 64:(n + 1) * 64], 0.0), axis=0, keepdims=True)
            lse_out[other] = jnp.broadcast_to(flat, (8, DH))

            @pl.when(other != line)
            def _():
                target = peer_device(other)
                send(part_out.at[pl.ds(other * 64, 64)], part_in.at[pl.ds(line * 64, 64)], s_part, r_part, target)
                send(lse_out.at[other], lse_in.at[line], s_lse, r_lse, target)
        return carry

    lax.fori_loop(0, 8, attend, 0)
    part_in[pl.ds(line * 64, 64), :] = part_out[pl.ds(line * 64, 64), :]
    lse_in[line] = lse_out[line]

    gather_wait(2)
    mine = anchor.at[pl.ds(half, 2048)]
    send(mine, mine, s_anc.at[4], r_anc.at[4], me + 1 - 2 * core)
    ones_first = jnp.where(row < valid_ref[0], 1.0, 0.0).astype(bf16)

    def anchor_block(i, carry):
        g = (4 * core + i) % 8

        @pl.when(i == MERGE_AT)
        def _():
            drain(part_in.at[pl.ds(0, 15 * 64)], r_part)
            drain(lse_in.at[pl.ds(0, 15)], r_lse)
            lse_all = lse_in[...]
            weight = jnp.exp2(lse_all - jnp.max(lse_all, axis=0, keepdims=True))
            weight = weight / jnp.sum(weight, axis=0, keepdims=True)
            merged = jnp.zeros((64, DH), f32)
            for j in range(16):
                column = jnp.sum(jnp.where(diag, weight[j, 0:1, :], 0.0), axis=1, keepdims=True)
                merged += column * part_in[j * 64:(j + 1) * 64, :].astype(f32)
            fin_out[...] = merged.reshape(8, 8, DH)

            def send_fin(d, carry):
                other = (member + d) % 8
                send(fin_out.at[other], fin_in.at[head], s_fin, r_fin, me - member + other)
                return carry

            lax.fori_loop(1, 8, send_fin, 0)
            fin_in[head] = fin_out[member]

        @pl.when(i == 4)
        def _():
            drain(anchor.at[pl.ds(0, 2048)], r_anc.at[4])

        base = pl.multiple_of(g * 512, 512)

        @pl.when(me != 0)
        def _():
            keys = anchor[pl.ds(base, 256), :]
            values = jnp.concatenate([anchor[pl.ds(base + 256, 256), :], ones_first], axis=1)
            for h in range(GROUP):
                cols = pl.ds(pl.multiple_of(g * GROUP * DH, GROUP * DH) + h * DH, DH)
                s = lax.dot_general(q_ref[:, cols], keys, NT, preferred_element_type=f32)
                lse = own_lse[:, cols]
                peak = jnp.maximum(jnp.max(s, axis=1, keepdims=True) * EXP2_SCALE, lse)
                p = jnp.concatenate(
                    [jnp.exp2(s[:, :DH] * EXP2_SCALE - peak), jnp.exp2(s[:, DH:] * EXP2_SCALE - peak)], axis=1).astype(bf16)
                o = jnp.dot(p, values, preferred_element_type=f32)
                scale = jnp.exp2(lse - peak)
                mixed = (o[:, :DH] + scale * own_out[:, cols]) / (o[:, DH:] + scale)
                out_ref[:, cols] = jnp.where(live, mixed, 0.0).astype(bf16)

        @pl.when(me == 0)
        def _():
            for h in range(GROUP):
                cols = pl.ds(pl.multiple_of(g * GROUP * DH, GROUP * DH) + h * DH, DH)
                out_ref[:, cols] = jnp.where(live, own_out[:, cols], 0.0).astype(bf16)

        return carry

    lax.fori_loop(0, KVH, anchor_block, 0)

    drain(fin_in.at[pl.ds(0, 7)], r_fin)
    answer_ref[...] = jnp.where(me < qlen_ref[0], fin_in[...].reshape(64, DH), 0.0)

    drain(rows_in.at[pl.ds(0, 7)], s_rows)
    drain(kvbuf.at[pl.ds(0, 7 * 512)], s_kv)
    drain(q_all.at[pl.ds(0, 15 * 64)], s_q)
    drain(part_in.at[pl.ds(0, 15 * 64)], s_part)
    drain(lse_in.at[pl.ds(0, 15)], s_lse)
    drain(fin_in.at[pl.ds(0, 7)], s_fin)
    for n in range(3):
        drain(anchor.at[pl.ds(0, 3 * sizes[n])], s_anc.at[n + 1])
    drain(anchor.at[pl.ds(0, 2048)], s_anc.at[4])

    @pl.when(me == 0)
    def _():
        drain(anchor.at[pl.ds(0, 63 * 32)], s_anc.at[0])
        drain(anchor.at[pl.ds(0, 2048)], s_anc.at[5])


def body(context_q, context_k, context_v, question, valid, qlen):
    hbm = pl.BlockSpec(memory_space=pltpu.HBM)
    vmem = pl.BlockSpec(memory_space=pltpu.VMEM)
    dma = pltpu.SemaphoreType.DMA
    encoded, answer = pl.pallas_call(
        star_kernel,
        out_shape=(jax.ShapeDtypeStruct((BLK, H * DH), bf16), jax.ShapeDtypeStruct((H, DH), f32)),
        in_specs=[hbm] * 5 + [pl.BlockSpec(memory_space=pltpu.SMEM)],
        out_specs=(vmem, vmem),
        scratch_shapes=[
            pltpu.VMEM((BLK, H * DH), bf16),
            pltpu.VMEM((BLK, KVH * DH), bf16),
            pltpu.VMEM((BLK, KVH * DH), bf16),
            pltpu.VMEM((1, H * DH), bf16),
            pltpu.SMEM((N,), jnp.int32),
            pltpu.VMEM((BLK, H * DH), f32),
            pltpu.VMEM((BLK, H * DH), f32),
            pltpu.VMEM((H, DH), f32),
            pltpu.VMEM((KVH * 512, DH), bf16),
            pltpu.VMEM((8 * 512, DH), bf16),
            pltpu.VMEM((8 * BLK, DH), bf16),
            pltpu.VMEM((8, 8, DH), f32),
            pltpu.VMEM((16 * 64, DH), bf16),
            pltpu.VMEM((16 * 64, DH), bf16),
            pltpu.VMEM((16, 8, DH), f32),
            pltpu.VMEM((16 * 64, DH), bf16),
            pltpu.VMEM((16, 8, DH), f32),
            pltpu.VMEM((8, 8, DH), f32),
            pltpu.VMEM((8, 8, DH), f32),
            pltpu.VMEM((KVH * 512, DH), bf16),
            dma((5,)), dma, dma, dma, dma, dma, dma, dma((6,)), dma((5,)), dma, dma, dma, dma, dma, dma, dma,
        ],
        compiler_params=pltpu.CompilerParams(collective_id=0, has_side_effects=True, vmem_limit_bytes=44 << 20),
        name="star",
    )(*[pltpu.with_memory_space_constraint(a, pltpu.HBM) for a in (context_q, context_k, context_v, question, valid)], qlen)
    return encoded, answer.reshape(1, H * DH).astype(bf16)


def solution(mesh):
    in_specs = (P("ctx", None), P("ctx", None), P("ctx", None), P("ctx", None), P(), P())
    out_specs = (P("ctx", None), P("ctx", None))
    return jax.shard_map(body, mesh=mesh, in_specs=in_specs, out_specs=out_specs, check_vma=False)
```

```python
import functools

import jax
import jax.numpy as jnp
from jax import lax
from jax.experimental import pallas as pl
from jax.experimental.pallas import tpu as pltpu
from jax.sharding import PartitionSpec as P

H = 64
KVH = 8
DH = 128
BLK = 256
N = 128
GROUP = H // KVH
EXP2_SCALE = 1.4426950408889634 * DH ** (-0.5)

f32 = jnp.float32
bf16 = jnp.bfloat16
MESH = pl.DeviceIdType.MESH
ORDER = (0, 1, 3, 2)
NT = (((1,), (1,)), ((), ()))

ROWS_AT = 1
SPREAD_AT = 2
GATHER_AT = 2
MERGE_AT = 3
GREETINGS = 9 + 1 + 15 + 7 + 7


def stride_of(axis):
    return 2 + 6 * axis + 9 * axis * (axis - 1)


def send(src, dst, send_sem, recv_sem, device):
    pltpu.make_async_remote_copy(
        src_ref=src, dst_ref=dst, send_sem=send_sem, recv_sem=recv_sem,
        device_id=(device,), device_id_type=MESH,
    ).start()


def drain(ref, sem):
    pltpu.make_async_copy(ref, ref, sem).wait()


def star_kernel(
    q_hbm, k_hbm, v_hbm, question_hbm, valid_hbm, qlen_ref,
    out_ref, answer_ref,
    q_ref, k_ref, v_ref, question_ref, valid_ref,
    own_out, own_lse, q64, kvs, kvbuf, ones, rows_in, q_all, part_out, lse_out, part_in, lse_in, fin_out, fin_in, anchor,
    load_sem, s_rows, r_rows, s_q, r_q, s_kv, r_kv, s_anc, r_anc, s_head, r_head, s_core, r_core, s_part, r_part, s_lse, r_lse, s_fin, r_fin, own_sem,
):
    me = lax.axis_index("ctx")
    core = me % 2
    x = (me // 2) % 4
    z = (me // 8) % 4
    y = me // 32
    cls = (x + y + z) % 4
    head = 2 * cls + core
    line = me // 8
    member = me % 8

    loads = [
        pltpu.make_async_copy(src, dst, load_sem.at[n])
        for n, (src, dst) in enumerate([
            (valid_hbm, valid_ref), (k_hbm, k_ref), (v_hbm, v_ref), (question_hbm, question_ref),
            (q_hbm, q_ref)])
    ]
    for load in loads:
        load.start()

    axis = head % 3
    stride = stride_of(axis)
    first = me - core - ((me // stride) % 4) * stride
    other_core = me + 1 - 2 * core

    st = (2 + 30 * core, 8 - 6 * core, 32 - 24 * core)
    at = [(me // step) % 4 for step in st]
    half = 2048 * core

    def along(n, d):
        return me + ((at[n] + d) % 4 - at[n]) * st[n]

    def peer_device(other):
        return (other * 4 + (cls + 8 - other // 4 - other % 4) % 4) * 2 + core

    def peer(d):
        other = (line + d) % 16
        return other, peer_device(other)

    barrier = pltpu.get_barrier_semaphore()

    def greet(device):
        pl.semaphore_signal(barrier, inc=1, device_id=(device,), device_id_type=MESH)

    @pl.when(jnp.logical_and(at[0] == 0, me != 0))
    def _():
        greet(0)

    for n in range(3):
        for d in (1, 2, 3):
            greet(along(n, d))
    greet(other_core)
    for d in range(1, 16):
        greet(peer(d)[1])
    for d in range(1, 8):
        greet(me - member + (member + d) % 8)
        source = ((me // stride) % 4 * 2 + core + d) % 8
        greet(first + source // 2 * stride + source % 2)

    for load in loads[:4]:
        load.wait()
    valid_here = valid_ref[me]
    row = lax.broadcasted_iota(jnp.int32, (BLK, DH), 0)
    live = row < valid_here
    for h in range(H):
        q64[h:h + 1, :] = question_ref[:, h * DH:(h + 1) * DH].astype(f32)
    for h in range(KVH):
        cols = slice(h * DH, (h + 1) * DH)
        k_h = k_ref[:, cols].astype(f32)
        v_h = v_ref[:, cols].astype(f32)
        kvs[h * 512:h * 512 + 256, :] = jnp.where(live, k_h, k_h[0:1, :]).astype(bf16)
        kvs[h * 512 + 256:h * 512 + 512, :] = jnp.where(live, v_h, 0.0).astype(bf16)
    @pl.when(me == 0)
    def _():
        pl.semaphore_wait(barrier, GREETINGS + 31)

    @pl.when(me != 0)
    def _():
        pl.semaphore_wait(barrier, GREETINGS)

    def send_rows(d, carry):
        other = (head + d) % 8
        target = me - member + ((other // 2 + 8 - y - z) % 4) * 2 + other % 2
        send(q64.at[pl.ds(other * 8, 8)], rows_in.at[member], s_rows, r_rows, target)
        return carry

    lax.fori_loop(1, 8, send_rows, 0)

    @pl.when(me == 0)
    def _():
        def scatter(j, carry):
            piece = 2048 + 128 * ((j % 4) * 4 + j // 4)
            send(kvs.at[pl.ds(piece, 128)], anchor.at[pl.ds(piece, 128)], s_anc.at[0], r_anc.at[0], 8 * (j % 4) + 2 * (j // 4) + 1)

            @pl.when(j != 0)
            def _():
                piece = 128 * j
                send(kvs.at[pl.ds(piece, 128)], anchor.at[pl.ds(piece, 128)], s_anc.at[3], r_anc.at[0], 8 * j)

            return carry

        lax.fori_loop(0, 16, scatter, 0)
        anchor[0:128, :] = kvs[0:128, :]

    def send_kv(d, carry):
        other = (head + d) % 8
        step = stride_of(other % 3)
        at = (me // step) % 4
        target = me - core + ((at + other // 2 + 4 - cls) % 4 - at) * step + other % 2
        send(kvs.at[pl.ds(other * 512, 512)], kvbuf.at[pl.ds((at * 2 + core) * 512, 512)], s_kv, r_kv, target)
        return carry

    at_home = (me // stride) % 4
    own_kv = pltpu.make_async_copy(
        kvs.at[pl.ds(head * 512, 512)], kvbuf.at[pl.ds((at_home * 2 + core) * 512, 512)], own_sem)
    own_kv.start()
    lax.fori_loop(1, 8, send_kv, 0)
    rows_in[member] = q64[pl.ds(head * 8, 8), :]
    for b in range(8):
        valid_b = valid_ref[first + (b // 2) * stride + b % 2]
        ones[b * BLK:(b + 1) * BLK, :] = jnp.where(row < valid_b, 1.0, 0.0).astype(bf16)

    spread_rows = pl.ds(half + 512 * at[2] + 128 * at[1], 128)

    def spread():
        @pl.when(at[0] == 0)
        def _():
            @pl.when(me != 0)
            def _():
                drain(anchor.at[pl.ds(0, 128)], r_anc.at[0])

            for d in (1, 2, 3):
                send(anchor.at[spread_rows], anchor.at[spread_rows], s_anc.at[1], r_anc.at[1], along(0, d))
            send_gather()

    def gather():
        @pl.when(at[0] != 0)
        def _():
            drain(anchor.at[pl.ds(0, 128)], r_anc.at[1])
            send_gather()

    def send_gather():
        for d in (1, 2, 3):
            send(anchor.at[spread_rows], anchor.at[spread_rows], s_anc.at[2], r_anc.at[2], along(1, d))

    def own_head(j):
        return 4 * core + (at[2] + ORDER[j]) % 4

    def share(j):
        rows = anchor.at[pl.ds(own_head(j) * 512, 512)]
        send(rows, rows, s_core.at[j], r_core.at[j], other_core)

    def gather_heads():
        drain(anchor.at[pl.ds(0, 3 * 128)], r_anc.at[2])
        share(0)
        rows = anchor.at[pl.ds(own_head(0) * 512, 512)]
        for j in (1, 2, 3):
            send(rows, rows, s_head.at[j], r_head.at[j], along(2, 4 - ORDER[j]))

    def pass_on(j):
        drain(anchor.at[pl.ds(0, 512)], r_head.at[j])
        share(j)

    loads[4].wait()
    causal = lax.broadcasted_iota(jnp.int32, (BLK, BLK), 1) <= lax.broadcasted_iota(jnp.int32, (BLK, BLK), 0)
    ones_own = jnp.where(live, 1.0, 0.0).astype(bf16)

    def own_block(n, carry):
        @pl.when(n == ROWS_AT)
        def _():
            drain(rows_in.at[pl.ds(0, 7)], r_rows)
            q_all[pl.ds(line * 64, 64), :] = rows_in[...].reshape(64, DH).astype(bf16)

            def send_q(d, carry):
                other, target = peer(d)
                send(q_all.at[pl.ds(line * 64, 64)], q_all.at[pl.ds(line * 64, 64)], s_q, r_q, target)
                return carry

            lax.fori_loop(1, 16, send_q, 0)

        pl.when(n == SPREAD_AT)(spread)
        for g in (2 * n, 2 * n + 1):
            base = pl.multiple_of(g * 512, 512)
            keys = kvs[pl.ds(base, 256), :]
            values = jnp.concatenate([kvs[pl.ds(base + 256, 256), :], ones_own], axis=1)
            for h in range(GROUP):
                cols = pl.ds(pl.multiple_of(g * GROUP * DH, GROUP * DH) + h * DH, DH)
                s = lax.dot_general(q_ref[:, cols], keys, NT, preferred_element_type=f32)
                s = jnp.where(causal, s, -1e30)
                peak = jnp.max(s, axis=1, keepdims=True) * EXP2_SCALE
                p = jnp.exp2(s * EXP2_SCALE - peak).astype(bf16)
                o = jnp.dot(p, values, preferred_element_type=f32)
                own_out[:, cols] = o[:, :DH] / o[:, DH:]
                own_lse[:, cols] = peak + jnp.log2(o[:, DH:])
        return carry

    lax.fori_loop(0, KVH // 2, own_block, 0)

    gather()

    drain(q_all.at[pl.ds(0, 15 * 64)], r_q)
    own_kv.wait()
    drain(kvbuf.at[pl.ds(0, 7 * 512)], r_kv)

    diag = lax.broadcasted_iota(jnp.int32, (64, DH), 0) == lax.broadcasted_iota(jnp.int32, (64, DH), 1)

    def attend(i, carry):
        pl.when(i == GATHER_AT)(gather_heads)
        chunk = (i + line // 4) % 4
        rows = pl.ds(pl.multiple_of(chunk * 256, 256), 256)
        q = q_all[rows, :]
        peak = None
        for b in range(0, 8, 2):
            keys = jnp.concatenate([kvbuf[n * 512:n * 512 + 256, :] for n in (b, b + 1)], axis=0)
            values = jnp.concatenate(
                [jnp.concatenate([kvbuf[n * 512 + 256:n * 512 + 512, :], ones[n * BLK:(n + 1) * BLK, :]], axis=1) for n in (b, b + 1)],
                axis=0)
            s = lax.dot_general(q, keys, NT, preferred_element_type=f32)
            new_peak = jnp.max(s, axis=1, keepdims=True) * EXP2_SCALE
            if peak is not None:
                new_peak = jnp.maximum(peak, new_peak)
            p = jnp.exp2(s * EXP2_SCALE - new_peak).astype(bf16)
            o_b = jnp.dot(p, values, preferred_element_type=f32)
            o = o_b if peak is None else o * jnp.exp2(peak - new_peak) + o_b
            peak = new_peak
        total = o[:, DH:]
        part_out[rows, :] = (o[:, :DH] / total).astype(bf16)
        lse = peak + jnp.log2(total)
        for n in range(4):
            other = 4 * chunk + n
            flat = jnp.sum(jnp.where(diag, lse[n * 64:(n + 1) * 64], 0.0), axis=0, keepdims=True)
            lse_out[other] = jnp.broadcast_to(flat, (8, DH))

            @pl.when(other != line)
            def _():
                target = peer_device(other)
                send(part_out.at[pl.ds(other * 64, 64)], part_in.at[pl.ds(line * 64, 64)], s_part, r_part, target)
                send(lse_out.at[other], lse_in.at[line], s_lse, r_lse, target)
        return carry

    lax.fori_loop(0, 4, attend, 0)
    part_in[pl.ds(line * 64, 64), :] = part_out[pl.ds(line * 64, 64), :]
    lse_in[line] = lse_out[line]

    ones_first = jnp.where(row < valid_ref[0], 1.0, 0.0).astype(bf16)

    def anchor_block(i, carry):
        is_1, is_2, is_3 = i * (2 - i) * (3 - i) // 2, i * (i - 1) * (3 - i) // 2, i * (i - 1) * (i - 2) // 6
        core_a, core_b = (core + is_2) % 2, (core + 1 - is_1) % 2
        far_a, far_b = is_1 + is_2 + 2 * is_3, 3 * (is_1 + is_2) + 2 * is_3

        def head_at(c, far):
            return 4 * c + (c * z + (1 - c) * y + far) % 4

        @pl.when(i == 0)
        def _():
            drain(anchor.at[pl.ds(0, 512)], r_core.at[0])

        @pl.when(i == 1)
        def _():
            pass_on(1)
            pass_on(2)

        @pl.when(i == 2)
        def _():
            pass_on(3)
            drain(anchor.at[pl.ds(0, 512)], r_core.at[1])
            drain(anchor.at[pl.ds(0, 512)], r_core.at[2])

        @pl.when(i == 3)
        def _():
            drain(anchor.at[pl.ds(0, 512)], r_core.at[3])

        @pl.when(i == MERGE_AT)
        def _():
            drain(part_in.at[pl.ds(0, 15 * 64)], r_part)
            drain(lse_in.at[pl.ds(0, 15)], r_lse)
            lse_all = lse_in[...]
            weight = jnp.exp2(lse_all - jnp.max(lse_all, axis=0, keepdims=True))
            weight = weight / jnp.sum(weight, axis=0, keepdims=True)
            merged = jnp.zeros((64, DH), f32)
            for j in range(16):
                column = jnp.sum(jnp.where(diag, weight[j, 0:1, :], 0.0), axis=1, keepdims=True)
                merged += column * part_in[j * 64:(j + 1) * 64, :].astype(f32)
            fin_out[...] = merged.reshape(8, 8, DH)

            def send_fin(d, carry):
                other = (member + d) % 8
                send(fin_out.at[other], fin_in.at[head], s_fin, r_fin, me - member + other)
                return carry

            lax.fori_loop(1, 8, send_fin, 0)
            fin_in[head] = fin_out[member]

        groups = (head_at(core_a, far_a), head_at(core_b, far_b))

        @pl.when(me != 0)
        def _():
            for g in groups:
                base = pl.multiple_of(g * 512, 512)
                keys = anchor[pl.ds(base, 256), :]
                values = jnp.concatenate([anchor[pl.ds(base + 256, 256), :], ones_first], axis=1)
                for h in range(GROUP):
                    cols = pl.ds(pl.multiple_of(g * GROUP * DH, GROUP * DH) + h * DH, DH)
                    s = lax.dot_general(q_ref[:, cols], keys, NT, preferred_element_type=f32)
                    lse = own_lse[:, cols]
                    peak = jnp.maximum(jnp.max(s, axis=1, keepdims=True) * EXP2_SCALE, lse)
                    p = jnp.concatenate(
                        [jnp.exp2(s[:, :DH] * EXP2_SCALE - peak), jnp.exp2(s[:, DH:] * EXP2_SCALE - peak)], axis=1).astype(bf16)
                    o = jnp.dot(p, values, preferred_element_type=f32)
                    scale = jnp.exp2(lse - peak)
                    mixed = (o[:, :DH] + scale * own_out[:, cols]) / (o[:, DH:] + scale)
                    out_ref[:, cols] = jnp.where(live, mixed, 0.0).astype(bf16)

        @pl.when(me == 0)
        def _():
            for g in groups:
                for h in range(GROUP):
                    cols = pl.ds(pl.multiple_of(g * GROUP * DH, GROUP * DH) + h * DH, DH)
                    out_ref[:, cols] = jnp.where(live, own_out[:, cols], 0.0).astype(bf16)

        return carry

    lax.fori_loop(0, KVH // 2, anchor_block, 0)

    drain(fin_in.at[pl.ds(0, 7)], r_fin)
    answer_ref[...] = jnp.where(me < qlen_ref[0], fin_in[...].reshape(64, DH), 0.0)

    drain(rows_in.at[pl.ds(0, 7)], s_rows)
    drain(kvbuf.at[pl.ds(0, 7 * 512)], s_kv)
    drain(q_all.at[pl.ds(0, 15 * 64)], s_q)
    drain(part_in.at[pl.ds(0, 15 * 64)], s_part)
    drain(lse_in.at[pl.ds(0, 15)], s_lse)
    drain(fin_in.at[pl.ds(0, 7)], s_fin)
    drain(anchor.at[pl.ds(0, 3 * 128)], s_anc.at[2])
    for n in range(4):
        drain(anchor.at[pl.ds(0, 512)], s_core.at[n])
    for n in range(1, 4):
        drain(anchor.at[pl.ds(0, 512)], s_head.at[n])

    @pl.when(at[0] == 0)
    def _():
        drain(anchor.at[pl.ds(0, 3 * 128)], s_anc.at[1])

    @pl.when(me == 0)
    def _():
        drain(anchor.at[pl.ds(0, 2048)], s_anc.at[0])
        drain(anchor.at[pl.ds(0, 15 * 128)], s_anc.at[3])


def body(context_q, context_k, context_v, question, valid, qlen):
    hbm = pl.BlockSpec(memory_space=pltpu.HBM)
    vmem = pl.BlockSpec(memory_space=pltpu.VMEM)
    dma = pltpu.SemaphoreType.DMA
    encoded, answer = pl.pallas_call(
        star_kernel,
        out_shape=(jax.ShapeDtypeStruct((BLK, H * DH), bf16), jax.ShapeDtypeStruct((H, DH), f32)),
        in_specs=[hbm] * 5 + [pl.BlockSpec(memory_space=pltpu.SMEM)],
        out_specs=(vmem, vmem),
        scratch_shapes=[
            pltpu.VMEM((BLK, H * DH), bf16),
            pltpu.VMEM((BLK, KVH * DH), bf16),
            pltpu.VMEM((BLK, KVH * DH), bf16),
            pltpu.VMEM((1, H * DH), bf16),
            pltpu.SMEM((N,), jnp.int32),
            pltpu.VMEM((BLK, H * DH), f32),
            pltpu.VMEM((BLK, H * DH), f32),
            pltpu.VMEM((H, DH), f32),
            pltpu.VMEM((KVH * 512, DH), bf16),
            pltpu.VMEM((8 * 512, DH), bf16),
            pltpu.VMEM((8 * BLK, DH), bf16),
            pltpu.VMEM((8, 8, DH), f32),
            pltpu.VMEM((16 * 64, DH), bf16),
            pltpu.VMEM((16 * 64, DH), bf16),
            pltpu.VMEM((16, 8, DH), f32),
            pltpu.VMEM((16 * 64, DH), bf16),
            pltpu.VMEM((16, 8, DH), f32),
            pltpu.VMEM((8, 8, DH), f32),
            pltpu.VMEM((8, 8, DH), f32),
            pltpu.VMEM((KVH * 512, DH), bf16),
            dma((5,)), dma, dma, dma, dma, dma, dma, dma((4,)), dma((3,)), dma((4,)), dma((4,)), dma((4,)), dma((4,)), dma, dma, dma, dma, dma, dma, dma,
        ],
        compiler_params=pltpu.CompilerParams(collective_id=0, has_side_effects=True, vmem_limit_bytes=44 << 20),
        name="star",
    )(*[pltpu.with_memory_space_constraint(a, pltpu.HBM) for a in (context_q, context_k, context_v, question, valid)], qlen)
    return encoded, answer.reshape(1, H * DH).astype(bf16)


def solution(mesh):
    in_specs = (P("ctx", None), P("ctx", None), P("ctx", None), P("ctx", None), P(), P())
    out_specs = (P("ctx", None), P("ctx", None))
    return jax.shard_map(body, mesh=mesh, in_specs=in_specs, out_specs=out_specs, check_vma=False)
```

```python
import functools

import jax
import jax.numpy as jnp
from jax import lax
from jax.experimental import pallas as pl
from jax.experimental.pallas import tpu as pltpu
from jax.sharding import PartitionSpec as P

H = 64
KVH = 8
DH = 128
BLK = 256
N = 128
GROUP = H // KVH
EXP2_SCALE = 1.4426950408889634 * DH ** (-0.5)

f32 = jnp.float32
bf16 = jnp.bfloat16
MESH = pl.DeviceIdType.MESH
ORDER = (0, 1, 3, 2)
NT = (((1,), (1,)), ((), ()))

ROWS_AT = 2
SPREAD_AT = 2
GATHER_AT = 2
MERGE_AT = 2
GREETINGS = 9 + 1 + 15 + 7 + 7


def stride_of(axis):
    return 2 + 6 * axis + 9 * axis * (axis - 1)


def send(src, dst, send_sem, recv_sem, device):
    pltpu.make_async_remote_copy(
        src_ref=src, dst_ref=dst, send_sem=send_sem, recv_sem=recv_sem,
        device_id=(device,), device_id_type=MESH,
    ).start()


def drain(ref, sem):
    pltpu.make_async_copy(ref, ref, sem).wait()


def star_kernel(
    q_hbm, k_hbm, v_hbm, question_hbm, valid_hbm, qlen_ref,
    out_ref, answer_ref,
    q_ref, k_ref, v_ref, question_ref, valid_ref,
    own_out, own_lse, q64, kvs, kvbuf, ones, rows_in, q_all, part_out, lse_out, part_in, lse_in, fin_out, fin_in, anchor,
    load_sem, s_rows, r_rows, s_q, r_q, s_kv, r_kv, s_anc, r_anc, s_head, r_head, s_core, r_core, s_part, r_part, s_lse, r_lse, s_fin, r_fin, own_sem,
):
    me = lax.axis_index("ctx")
    core = me % 2
    x = (me // 2) % 4
    z = (me // 8) % 4
    y = me // 32
    cls = (x + y + z) % 4
    head = 2 * cls + core
    line = me // 8
    member = me % 8

    axis = head % 3
    stride = stride_of(axis)
    first = me - core - ((me // stride) % 4) * stride
    other_core = me + 1 - 2 * core

    st = (2 + 30 * core, 8 - 6 * core, 32 - 24 * core)
    at = [(me // step) % 4 for step in st]
    half = 2048 * core

    def along(n, d):
        return me + ((at[n] + d) % 4 - at[n]) * st[n]

    def peer_device(other):
        return (other * 4 + (cls + 8 - other // 4 - other % 4) % 4) * 2 + core

    def peer(d):
        other = (line + d) % 16
        return other, peer_device(other)

    barrier = pltpu.get_barrier_semaphore()

    def greet(device):
        pl.semaphore_signal(barrier, inc=1, device_id=(device,), device_id_type=MESH)

    @pl.when(jnp.logical_and(at[0] == 0, me != 0))
    def _():
        greet(0)

    for n in range(3):
        for d in (1, 2, 3):
            greet(along(n, d))
    greet(other_core)
    for d in range(1, 16):
        greet(peer(d)[1])
    for d in range(1, 8):
        greet(me - member + (member + d) % 8)
        source = ((me // stride) % 4 * 2 + core + d) % 8
        greet(first + source // 2 * stride + source % 2)

    loads = [
        pltpu.make_async_copy(src, dst, load_sem.at[n])
        for n, (src, dst) in enumerate([
            (valid_hbm, valid_ref), (k_hbm, k_ref), (v_hbm, v_ref), (question_hbm, question_ref),
            (q_hbm, q_ref)])
    ]
    for load in loads:
        load.start()

    for load in loads[:4]:
        load.wait()
    valid_here = valid_ref[me]
    row = lax.broadcasted_iota(jnp.int32, (BLK, DH), 0)
    live = row < valid_here
    for h in range(H):
        q64[h:h + 1, :] = question_ref[:, h * DH:(h + 1) * DH].astype(f32)
    for h in range(KVH):
        cols = slice(h * DH, (h + 1) * DH)
        k_h = k_ref[:, cols].astype(f32)
        v_h = v_ref[:, cols].astype(f32)
        kvs[h * 512:h * 512 + 256, :] = jnp.where(live, k_h, k_h[0:1, :]).astype(bf16)
        kvs[h * 512 + 256:h * 512 + 512, :] = jnp.where(live, v_h, 0.0).astype(bf16)
    @pl.when(me == 0)
    def _():
        pl.semaphore_wait(barrier, GREETINGS + 31)

    @pl.when(me != 0)
    def _():
        pl.semaphore_wait(barrier, GREETINGS)

    def send_rows(d, carry):
        other = (head + d) % 8
        target = me - member + ((other // 2 + 8 - y - z) % 4) * 2 + other % 2
        send(q64.at[pl.ds(other * 8, 8)], rows_in.at[member], s_rows, r_rows, target)
        return carry

    lax.fori_loop(1, 8, send_rows, 0)

    spread_rows = pl.ds(half + 512 * at[2] + 128 * at[1], 128)

    def send_spread():
        for d in (1, 2, 3):
            send(anchor.at[spread_rows], anchor.at[spread_rows], s_anc.at[1], r_anc.at[1], along(0, d))
        send_gather()

    def spread():
        @pl.when(jnp.logical_and(at[0] == 0, me != 0))
        def _():
            drain(anchor.at[pl.ds(0, 128)], r_anc.at[0])
            send_spread()

    def gather():
        @pl.when(at[0] != 0)
        def _():
            drain(anchor.at[pl.ds(0, 128)], r_anc.at[1])
            send_gather()

    def send_gather():
        for d in (1, 2, 3):
            send(anchor.at[spread_rows], anchor.at[spread_rows], s_anc.at[2], r_anc.at[2], along(1, d))

    def own_head(j):
        return 4 * core + (at[2] + ORDER[j]) % 4

    def share(j):
        rows = anchor.at[pl.ds(own_head(j) * 512, 512)]
        send(rows, rows, s_core.at[j], r_core.at[j], other_core)

    def gather_heads():
        drain(anchor.at[pl.ds(0, 3 * 128)], r_anc.at[2])
        share(0)
        rows = anchor.at[pl.ds(own_head(0) * 512, 512)]
        for j in (1, 2, 3):
            send(rows, rows, s_head.at[j], r_head.at[j], along(2, 4 - ORDER[j]))

    def pass_on(j):
        drain(anchor.at[pl.ds(0, 512)], r_head.at[j])
        share(j)

    @pl.when(me == 0)
    def _():
        def scatter(i, carry):
            j = (i % 4) * 4 + (2 + 3 * (i // 4)) % 4
            piece = 2048 + 128 * ((j % 4) * 4 + j // 4)
            send(kvs.at[pl.ds(piece, 128)], anchor.at[pl.ds(piece, 128)], s_anc.at[0], r_anc.at[0], 8 * (j % 4) + 2 * (j // 4) + 1)

            @pl.when(j != 0)
            def _():
                piece = 128 * j
                send(kvs.at[pl.ds(piece, 128)], anchor.at[pl.ds(piece, 128)], s_anc.at[3], r_anc.at[0], 8 * j)

            return carry

        anchor[0:128, :] = kvs[0:128, :]
        lax.fori_loop(0, 16, scatter, 0)
        send_spread()

    def send_kv(d, carry):
        other = (head + d) % 8
        step = stride_of(other % 3)
        at = (me // step) % 4
        target = me - core + ((at + other // 2 + 4 - cls) % 4 - at) * step + other % 2
        send(kvs.at[pl.ds(other * 512, 512)], kvbuf.at[pl.ds((at * 2 + core) * 512, 512)], s_kv, r_kv, target)
        return carry

    at_home = (me // stride) % 4
    own_kv = pltpu.make_async_copy(
        kvs.at[pl.ds(head * 512, 512)], kvbuf.at[pl.ds((at_home * 2 + core) * 512, 512)], own_sem)
    own_kv.start()
    @pl.when(me > 1)
    def _():
        lax.fori_loop(1, 8, send_kv, 0)

    rows_in[member] = q64[pl.ds(head * 8, 8), :]
    for b in range(8):
        valid_b = valid_ref[first + (b // 2) * stride + b % 2]
        ones[b * BLK:(b + 1) * BLK, :] = jnp.where(row < valid_b, 1.0, 0.0).astype(bf16)

    loads[4].wait()
    causal = lax.broadcasted_iota(jnp.int32, (BLK, BLK), 1) <= lax.broadcasted_iota(jnp.int32, (BLK, BLK), 0)
    ones_own = jnp.where(live, 1.0, 0.0).astype(bf16)

    def own_block(n, carry):

        pl.when(n == SPREAD_AT)(spread)

        @pl.when(n == ROWS_AT)
        def _():
            drain(rows_in.at[pl.ds(0, 7)], r_rows)
            q_all[pl.ds(line * 64, 64), :] = rows_in[...].reshape(64, DH).astype(bf16)

            def send_q(d, carry):
                other, target = peer(d)
                send(q_all.at[pl.ds(line * 64, 64)], q_all.at[pl.ds(line * 64, 64)], s_q, r_q.at[y], target)
                return carry

            lax.fori_loop(1, 16, send_q, 0)


        @pl.when(n == 2)
        def _():
            @pl.when(me <= 1)
            def _():
                lax.fori_loop(1, 8, send_kv, 0)

        for g in (2 * n, 2 * n + 1):
            base = pl.multiple_of(g * 512, 512)
            keys = kvs[pl.ds(base, 256), :]
            values = jnp.concatenate([kvs[pl.ds(base + 256, 256), :], ones_own], axis=1)
            for h in range(GROUP):
                cols = pl.ds(pl.multiple_of(g * GROUP * DH, GROUP * DH) + h * DH, DH)
                s = lax.dot_general(q_ref[:, cols], keys, NT, preferred_element_type=f32)
                s = jnp.where(causal, s, -1e30)
                peak = jnp.max(s, axis=1, keepdims=True) * EXP2_SCALE
                p = jnp.exp2(s * EXP2_SCALE - peak).astype(bf16)
                o = jnp.dot(p, values, preferred_element_type=f32)
                own_out[:, cols] = o[:, :DH] * pl.reciprocal(o[:, DH:], approx=True)
                own_lse[:, cols] = peak + jnp.log2(o[:, DH:])
        return carry

    lax.fori_loop(0, KVH // 2, own_block, 0)

    gather()

    own_kv.wait()
    drain(kvbuf.at[pl.ds(0, 7 * 512)], r_kv)

    diag = lax.broadcasted_iota(jnp.int32, (64, DH), 0) == lax.broadcasted_iota(jnp.int32, (64, DH), 1)

    def attend(i, carry):
        pl.when(i == GATHER_AT)(gather_heads)
        chunk = (i + y) % 4

        @pl.when(i == 0)
        def _():
            drain(q_all.at[pl.ds(0, 3 * 64)], r_q.at[chunk])

        @pl.when(i != 0)
        def _():
            drain(q_all.at[pl.ds(0, 4 * 64)], r_q.at[chunk])

        rows = pl.ds(pl.multiple_of(chunk * 256, 256), 256)
        q = q_all[rows, :]
        peak = None
        for b in range(0, 8, 2):
            keys = jnp.concatenate([kvbuf[n * 512:n * 512 + 256, :] for n in (b, b + 1)], axis=0)
            values = jnp.concatenate(
                [jnp.concatenate([kvbuf[n * 512 + 256:n * 512 + 512, :], ones[n * BLK:(n + 1) * BLK, :]], axis=1) for n in (b, b + 1)],
                axis=0)
            s = lax.dot_general(q, keys, NT, preferred_element_type=f32)
            new_peak = jnp.max(s, axis=1, keepdims=True) * EXP2_SCALE
            if peak is not None:
                new_peak = jnp.maximum(peak, new_peak)
            p = jnp.exp2(s * EXP2_SCALE - new_peak).astype(bf16)
            o_b = jnp.dot(p, values, preferred_element_type=f32)
            o = o_b if peak is None else o * jnp.exp2(peak - new_peak) + o_b
            peak = new_peak
        total = o[:, DH:]
        part_out[rows, :] = (o[:, :DH] * pl.reciprocal(total, approx=True)).astype(bf16)
        lse = peak + jnp.log2(total)
        for n in range(4):
            other = 4 * chunk + n
            flat = jnp.sum(jnp.where(diag, lse[n * 64:(n + 1) * 64], 0.0), axis=0, keepdims=True)
            lse_out[other] = jnp.broadcast_to(flat, (8, DH))

            @pl.when(other != line)
            def _():
                target = peer_device(other)
                send(part_out.at[pl.ds(other * 64, 64)], part_in.at[pl.ds(line * 64, 64)], s_part, r_part, target)
                send(lse_out.at[other], lse_in.at[line], s_lse, r_lse, target)
        return carry

    lax.fori_loop(0, 4, attend, 0)
    part_in[pl.ds(line * 64, 64), :] = part_out[pl.ds(line * 64, 64), :]
    lse_in[line] = lse_out[line]

    ones_first = jnp.where(row < valid_ref[0], 1.0, 0.0).astype(bf16)

    def anchor_block(i, carry):
        is_1, is_2, is_3 = i * (2 - i) * (3 - i) // 2, i * (i - 1) * (3 - i) // 2, i * (i - 1) * (i - 2) // 6
        core_a, core_b = (core + is_2) % 2, (core + 1 - is_1) % 2
        far_a, far_b = is_1 + is_2 + 2 * is_3, 3 * (is_1 + is_2) + 2 * is_3

        def head_at(c, far):
            return 4 * c + (c * z + (1 - c) * y + far) % 4

        @pl.when(i == 0)
        def _():
            drain(anchor.at[pl.ds(0, 512)], r_core.at[0])

        @pl.when(i == 1)
        def _():
            pass_on(1)
            pass_on(2)

        @pl.when(i == 2)
        def _():
            pass_on(3)
            drain(anchor.at[pl.ds(0, 512)], r_core.at[1])
            drain(anchor.at[pl.ds(0, 512)], r_core.at[2])

        @pl.when(i == 3)
        def _():
            drain(anchor.at[pl.ds(0, 512)], r_core.at[3])

        @pl.when(i == MERGE_AT)
        def _():
            drain(part_in.at[pl.ds(0, 15 * 64)], r_part)
            drain(lse_in.at[pl.ds(0, 15)], r_lse)
            lse_all = lse_in[...]
            weight = jnp.exp2(lse_all - jnp.max(lse_all, axis=0, keepdims=True))
            weight = weight / jnp.sum(weight, axis=0, keepdims=True)
            merged = jnp.zeros((64, DH), f32)
            for j in range(16):
                column = jnp.sum(jnp.where(diag, weight[j, 0:1, :], 0.0), axis=1, keepdims=True)
                merged += column * part_in[j * 64:(j + 1) * 64, :].astype(f32)
            fin_out[...] = merged.reshape(8, 8, DH)

            def send_fin(d, carry):
                other = (member + d) % 8
                send(fin_out.at[other], fin_in.at[head], s_fin, r_fin, me - member + other)
                return carry

            lax.fori_loop(1, 8, send_fin, 0)
            fin_in[head] = fin_out[member]

        groups = (head_at(core_a, far_a), head_at(core_b, far_b))

        @pl.when(me != 0)
        def _():
            for g in groups:
                base = pl.multiple_of(g * 512, 512)
                keys = anchor[pl.ds(base, 256), :]
                values = jnp.concatenate([anchor[pl.ds(base + 256, 256), :], ones_first], axis=1)
                for h in range(GROUP):
                    cols = pl.ds(pl.multiple_of(g * GROUP * DH, GROUP * DH) + h * DH, DH)
                    s = lax.dot_general(q_ref[:, cols], keys, NT, preferred_element_type=f32)
                    lse = own_lse[:, cols]
                    peak = jnp.maximum(jnp.max(s, axis=1, keepdims=True) * EXP2_SCALE, lse)
                    p = jnp.concatenate(
                        [jnp.exp2(s[:, :DH] * EXP2_SCALE - peak), jnp.exp2(s[:, DH:] * EXP2_SCALE - peak)], axis=1).astype(bf16)
                    o = jnp.dot(p, values, preferred_element_type=f32)
                    scale = jnp.exp2(lse - peak)
                    mixed = (o[:, :DH] + scale * own_out[:, cols]) * pl.reciprocal(o[:, DH:] + scale, approx=True)
                    out_ref[:, cols] = jnp.where(live, mixed, 0.0).astype(bf16)

        @pl.when(me == 0)
        def _():
            for g in groups:
                for h in range(GROUP):
                    cols = pl.ds(pl.multiple_of(g * GROUP * DH, GROUP * DH) + h * DH, DH)
                    out_ref[:, cols] = jnp.where(live, own_out[:, cols], 0.0).astype(bf16)

        return carry

    lax.fori_loop(0, KVH // 2, anchor_block, 0)

    drain(fin_in.at[pl.ds(0, 7)], r_fin)
    answer_ref[...] = jnp.where(me < qlen_ref[0], fin_in[...].reshape(64, DH), 0.0)

    drain(rows_in.at[pl.ds(0, 7)], s_rows)
    drain(kvbuf.at[pl.ds(0, 7 * 512)], s_kv)
    drain(q_all.at[pl.ds(0, 15 * 64)], s_q)
    drain(part_in.at[pl.ds(0, 15 * 64)], s_part)
    drain(lse_in.at[pl.ds(0, 15)], s_lse)
    drain(fin_in.at[pl.ds(0, 7)], s_fin)
    drain(anchor.at[pl.ds(0, 3 * 128)], s_anc.at[2])
    for n in range(4):
        drain(anchor.at[pl.ds(0, 512)], s_core.at[n])
    for n in range(1, 4):
        drain(anchor.at[pl.ds(0, 512)], s_head.at[n])

    @pl.when(at[0] == 0)
    def _():
        drain(anchor.at[pl.ds(0, 3 * 128)], s_anc.at[1])

    @pl.when(me == 0)
    def _():
        drain(anchor.at[pl.ds(0, 2048)], s_anc.at[0])
        drain(anchor.at[pl.ds(0, 15 * 128)], s_anc.at[3])


def body(context_q, context_k, context_v, question, valid, qlen):
    hbm = pl.BlockSpec(memory_space=pltpu.HBM)
    vmem = pl.BlockSpec(memory_space=pltpu.VMEM)
    dma = pltpu.SemaphoreType.DMA
    encoded, answer = pl.pallas_call(
        star_kernel,
        out_shape=(jax.ShapeDtypeStruct((BLK, H * DH), bf16), jax.ShapeDtypeStruct((H, DH), f32)),
        in_specs=[hbm] * 5 + [pl.BlockSpec(memory_space=pltpu.SMEM)],
        out_specs=(vmem, vmem),
        scratch_shapes=[
            pltpu.VMEM((BLK, H * DH), bf16),
            pltpu.VMEM((BLK, KVH * DH), bf16),
            pltpu.VMEM((BLK, KVH * DH), bf16),
            pltpu.VMEM((1, H * DH), bf16),
            pltpu.SMEM((N,), jnp.int32),
            pltpu.VMEM((BLK, H * DH), f32),
            pltpu.VMEM((BLK, H * DH), f32),
            pltpu.VMEM((H, DH), f32),
            pltpu.VMEM((KVH * 512, DH), bf16),
            pltpu.VMEM((8 * 512, DH), bf16),
            pltpu.VMEM((8 * BLK, DH), bf16),
            pltpu.VMEM((8, 8, DH), f32),
            pltpu.VMEM((16 * 64, DH), bf16),
            pltpu.VMEM((16 * 64, DH), bf16),
            pltpu.VMEM((16, 8, DH), f32),
            pltpu.VMEM((16 * 64, DH), bf16),
            pltpu.VMEM((16, 8, DH), f32),
            pltpu.VMEM((8, 8, DH), f32),
            pltpu.VMEM((8, 8, DH), f32),
            pltpu.VMEM((KVH * 512, DH), bf16),
            dma((5,)), dma, dma, dma, dma((4,)), dma, dma, dma((4,)), dma((3,)), dma((4,)), dma((4,)), dma((4,)), dma((4,)), dma, dma, dma, dma, dma, dma, dma,
        ],
        compiler_params=pltpu.CompilerParams(collective_id=0, has_side_effects=True, vmem_limit_bytes=44 << 20),
        name="star",
    )(*[pltpu.with_memory_space_constraint(a, pltpu.HBM) for a in (context_q, context_k, context_v, question, valid)], qlen)
    return encoded, answer.reshape(1, H * DH).astype(bf16)


def solution(mesh):
    in_specs = (P("ctx", None), P("ctx", None), P("ctx", None), P("ctx", None), P(), P())
    out_specs = (P("ctx", None), P("ctx", None))
    return jax.shard_map(body, mesh=mesh, in_specs=in_specs, out_specs=out_specs, check_vma=False)
```

```python
import functools

import jax
import jax.numpy as jnp
from jax import lax
from jax.experimental import pallas as pl
from jax.experimental.pallas import tpu as pltpu
from jax.sharding import PartitionSpec as P

H = 64
KVH = 8
DH = 128
BLK = 256
N = 128
GROUP = H // KVH
EXP2_SCALE = 1.4426950408889634 * DH ** (-0.5)

f32 = jnp.float32
bf16 = jnp.bfloat16
MESH = pl.DeviceIdType.MESH
DEAD = 1e30
ORDER = (0, 1, 3, 2)
NT = (((1,), (1,)), ((), ()))

ROWS_AT = 2
SPREAD_AT = 2
GATHER_AT = 2
MERGE_AT = 2
GREETINGS = 9 + 1 + 15 + 7 + 7


def stride_of(axis):
    return 2 + 6 * axis + 9 * axis * (axis - 1)


def send(src, dst, send_sem, recv_sem, device):
    pltpu.make_async_remote_copy(
        src_ref=src, dst_ref=dst, send_sem=send_sem, recv_sem=recv_sem,
        device_id=(device,), device_id_type=MESH,
    ).start()


def drain(ref, sem):
    pltpu.make_async_copy(ref, ref, sem).wait()


def star_kernel(
    q_hbm, k_hbm, v_hbm, question_hbm, valid_hbm, qlen_ref,
    out_ref, answer_ref,
    q_ref, k_ref, v_ref, question_ref, valid_ref,
    own_out, own_lse, q64, kvs, kvbuf, ones, rows_in, q_all, part_out, lse_out, part_in, lse_in, fin_out, fin_in, anchor,
    load_sem, s_rows, r_rows, s_q, r_q, s_kv, r_kv, s_anc, r_anc, s_head, r_head, s_core, r_core, s_part, r_part, s_lse, r_lse, s_fin, r_fin, own_sem,
):
    me = lax.axis_index("ctx")
    core = me % 2
    x = (me // 2) % 4
    z = (me // 8) % 4
    y = me // 32
    cls = (x + y + z) % 4
    head = 2 * cls + core
    line = me // 8
    member = me % 8

    axis = head % 3
    stride = stride_of(axis)
    first = me - core - ((me // stride) % 4) * stride
    other_core = me + 1 - 2 * core

    st = (2 + 30 * core, 8 - 6 * core, 32 - 24 * core)
    at = [(me // step) % 4 for step in st]
    half = 2048 * core

    def along(n, d):
        return me + ((at[n] + d) % 4 - at[n]) * st[n]

    def peer_device(other):
        return (other * 4 + (cls + 8 - other // 4 - other % 4) % 4) * 2 + core

    def peer(d):
        other = (line + d) % 16
        return other, peer_device(other)

    barrier = pltpu.get_barrier_semaphore()

    def greet(device):
        pl.semaphore_signal(barrier, inc=1, device_id=(device,), device_id_type=MESH)

    @pl.when(jnp.logical_and(at[0] == 0, me != 0))
    def _():
        greet(0)

    for n in range(3):
        for d in (1, 2, 3):
            greet(along(n, d))
    greet(other_core)
    for d in range(1, 16):
        greet(peer(d)[1])
    for d in range(1, 8):
        greet(me - member + (member + d) % 8)
        source = ((me // stride) % 4 * 2 + core + d) % 8
        greet(first + source // 2 * stride + source % 2)

    loads = [
        pltpu.make_async_copy(src, dst, load_sem.at[n])
        for n, (src, dst) in enumerate([
            (valid_hbm, valid_ref), (k_hbm, k_ref), (v_hbm, v_ref), (question_hbm, question_ref),
            (q_hbm, q_ref)])
    ]
    for load in loads:
        load.start()

    for load in loads[:4]:
        load.wait()
    valid_here = valid_ref[me]
    row = lax.broadcasted_iota(jnp.int32, (BLK, DH), 0)
    live = row < valid_here
    for h in range(H):
        q64[h:h + 1, :] = question_ref[:, h * DH:(h + 1) * DH].astype(f32)
    for h in range(KVH):
        cols = slice(h * DH, (h + 1) * DH)
        k_h = k_ref[:, cols].astype(f32)
        v_h = v_ref[:, cols].astype(f32)
        kvs[h * 512:h * 512 + 256, :] = jnp.where(live, k_h, k_h[0:1, :]).astype(bf16)
        kvs[h * 512 + 256:h * 512 + 512, :] = jnp.where(live, v_h, 0.0).astype(bf16)
    @pl.when(me == 0)
    def _():
        pl.semaphore_wait(barrier, GREETINGS + 31)

    @pl.when(me != 0)
    def _():
        pl.semaphore_wait(barrier, GREETINGS)

    def send_rows(d, carry):
        other = (head + d) % 8
        target = me - member + ((other // 2 + 8 - y - z) % 4) * 2 + other % 2
        send(q64.at[pl.ds(other * 8, 8)], rows_in.at[member], s_rows, r_rows, target)
        return carry

    lax.fori_loop(1, 8, send_rows, 0)

    spread_rows = pl.ds(half + 512 * at[2] + 128 * at[1], 128)

    def send_spread():
        for d in (1, 2, 3):
            send(anchor.at[spread_rows], anchor.at[spread_rows], s_anc.at[1], r_anc.at[1], along(0, d))
        send_gather()

    def spread():
        @pl.when(jnp.logical_and(at[0] == 0, me != 0))
        def _():
            drain(anchor.at[pl.ds(0, 128)], r_anc.at[0])
            send_spread()

    def gather():
        @pl.when(at[0] != 0)
        def _():
            drain(anchor.at[pl.ds(0, 128)], r_anc.at[1])
            send_gather()

    def send_gather():
        for d in (1, 2, 3):
            send(anchor.at[spread_rows], anchor.at[spread_rows], s_anc.at[2], r_anc.at[2], along(1, d))

    def own_head(j):
        return 4 * core + (at[2] + ORDER[j]) % 4

    def share(j):
        rows = anchor.at[pl.ds(own_head(j) * 512, 512)]
        send(rows, rows, s_core.at[j], r_core.at[j], other_core)

    def gather_heads():
        drain(anchor.at[pl.ds(0, 3 * 128)], r_anc.at[2])
        share(0)
        rows = anchor.at[pl.ds(own_head(0) * 512, 512)]
        for j in (1, 2, 3):
            send(rows, rows, s_head.at[j], r_head.at[j], along(2, 4 - ORDER[j]))

    def pass_on(j):
        drain(anchor.at[pl.ds(0, 512)], r_head.at[j])
        share(j)

    @pl.when(me == 0)
    def _():
        def scatter(i, carry):
            j = ((i + 2) % 4) * 4 + (2 + 3 * (i // 4)) % 4
            piece = 2048 + 128 * ((j % 4) * 4 + j // 4)
            send(kvs.at[pl.ds(piece, 128)], anchor.at[pl.ds(piece, 128)], s_anc.at[0], r_anc.at[0], 8 * (j % 4) + 2 * (j // 4) + 1)

            @pl.when(j != 0)
            def _():
                piece = 128 * j
                send(kvs.at[pl.ds(piece, 128)], anchor.at[pl.ds(piece, 128)], s_anc.at[3], r_anc.at[0], 8 * j)

            return carry

        anchor[0:128, :] = kvs[0:128, :]
        lax.fori_loop(0, 16, scatter, 0)
        send_spread()

    def send_kv(d, carry):
        other = (head + d) % 8
        step = stride_of(other % 3)
        at = (me // step) % 4
        target = me - core + ((at + other // 2 + 4 - cls) % 4 - at) * step + other % 2
        send(kvs.at[pl.ds(other * 512, 512)], kvbuf.at[pl.ds((at * 2 + core) * 512, 512)], s_kv, r_kv, target)
        return carry

    at_home = (me // stride) % 4
    own_kv = pltpu.make_async_copy(
        kvs.at[pl.ds(head * 512, 512)], kvbuf.at[pl.ds((at_home * 2 + core) * 512, 512)], own_sem)
    own_kv.start()
    @pl.when(me > 1)
    def _():
        lax.fori_loop(1, 8, send_kv, 0)

    rows_in[member] = q64[pl.ds(head * 8, 8), :]
    for b in range(8):
        valid_b = valid_ref[first + (b // 2) * stride + b % 2]
        ones[b * BLK:(b + 1) * BLK, :] = jnp.where(row < valid_b, 1.0, 0.0).astype(bf16)

    loads[4].wait()
    causal = lax.broadcasted_iota(jnp.int32, (BLK, BLK), 1) <= lax.broadcasted_iota(jnp.int32, (BLK, BLK), 0)
    ones_own = jnp.where(live, 1.0, 0.0).astype(bf16)

    def own_block(n, carry):

        pl.when(n == SPREAD_AT)(spread)

        @pl.when(n == ROWS_AT)
        def _():
            drain(rows_in.at[pl.ds(0, 7)], r_rows)
            q_all[pl.ds(line * 64, 64), :] = rows_in[...].reshape(64, DH).astype(bf16)

            def send_q(d, carry):
                other, target = peer(d)
                send(q_all.at[pl.ds(line * 64, 64)], q_all.at[pl.ds(line * 64, 64)], s_q, r_q.at[y], target)
                return carry

            lax.fori_loop(1, 16, send_q, 0)


        @pl.when(n == 2)
        def _():
            @pl.when(me <= 1)
            def _():
                lax.fori_loop(1, 8, send_kv, 0)

        for g in (2 * n, 2 * n + 1):
            base = pl.multiple_of(g * 512, 512)
            keys = kvs[pl.ds(base, 256), :]
            values = jnp.concatenate([kvs[pl.ds(base + 256, 256), :], ones_own], axis=1)
            for h in range(GROUP):
                cols = pl.ds(pl.multiple_of(g * GROUP * DH, GROUP * DH) + h * DH, DH)
                s = lax.dot_general(q_ref[:, cols], keys, NT, preferred_element_type=f32)
                s = jnp.where(causal, s, -1e30)
                peak = jnp.max(s, axis=1, keepdims=True) * EXP2_SCALE
                p = jnp.exp2(s * EXP2_SCALE - peak).astype(bf16)
                o = jnp.dot(p, values, preferred_element_type=f32)
                own_out[:, cols] = jnp.where(live, o[:, :DH] * pl.reciprocal(o[:, DH:], approx=True), 0.0)
                own_lse[:, cols] = jnp.where(live, peak + jnp.log2(o[:, DH:]), DEAD)
        return carry

    lax.fori_loop(0, KVH // 2, own_block, 0)

    gather()

    own_kv.wait()
    drain(kvbuf.at[pl.ds(0, 7 * 512)], r_kv)

    diag = lax.broadcasted_iota(jnp.int32, (64, DH), 0) == lax.broadcasted_iota(jnp.int32, (64, DH), 1)

    def attend(i, carry):
        pl.when(i == GATHER_AT)(gather_heads)
        chunk = (i + y) % 4

        @pl.when(i == 0)
        def _():
            drain(q_all.at[pl.ds(0, 3 * 64)], r_q.at[chunk])

        @pl.when(i != 0)
        def _():
            drain(q_all.at[pl.ds(0, 4 * 64)], r_q.at[chunk])

        rows = pl.ds(pl.multiple_of(chunk * 256, 256), 256)
        q = q_all[rows, :]
        peak = None
        for b in range(0, 8, 2):
            keys = jnp.concatenate([kvbuf[n * 512:n * 512 + 256, :] for n in (b, b + 1)], axis=0)
            values = jnp.concatenate(
                [jnp.concatenate([kvbuf[n * 512 + 256:n * 512 + 512, :], ones[n * BLK:(n + 1) * BLK, :]], axis=1) for n in (b, b + 1)],
                axis=0)
            s = lax.dot_general(q, keys, NT, preferred_element_type=f32)
            new_peak = jnp.max(s, axis=1, keepdims=True) * EXP2_SCALE
            if peak is not None:
                new_peak = jnp.maximum(peak, new_peak)
            p = jnp.exp2(s * EXP2_SCALE - new_peak).astype(bf16)
            o_b = jnp.dot(p, values, preferred_element_type=f32)
            o = o_b if peak is None else o * jnp.exp2(peak - new_peak) + o_b
            peak = new_peak
        total = o[:, DH:]
        part_out[rows, :] = (o[:, :DH] * pl.reciprocal(total, approx=True)).astype(bf16)
        lse = peak + jnp.log2(total)
        for n in range(4):
            other = 4 * chunk + n
            flat = jnp.sum(jnp.where(diag, lse[n * 64:(n + 1) * 64], 0.0), axis=0, keepdims=True)
            lse_out[other] = jnp.broadcast_to(flat, (8, DH))

            @pl.when(other != line)
            def _():
                target = peer_device(other)
                send(part_out.at[pl.ds(other * 64, 64)], part_in.at[pl.ds(line * 64, 64)], s_part, r_part, target)
                send(lse_out.at[other], lse_in.at[line], s_lse, r_lse, target)
        return carry

    lax.fori_loop(0, 4, attend, 0)
    part_in[pl.ds(line * 64, 64), :] = part_out[pl.ds(line * 64, 64), :]
    lse_in[line] = lse_out[line]

    ones_first = jnp.where(row < valid_ref[0], 1.0, 0.0).astype(bf16)

    def anchor_block(i, carry):
        is_1, is_2, is_3 = i * (2 - i) * (3 - i) // 2, i * (i - 1) * (3 - i) // 2, i * (i - 1) * (i - 2) // 6
        core_a, core_b = (core + is_2) % 2, (core + 1 - is_1) % 2
        far_a, far_b = is_1 + is_2 + 2 * is_3, 3 * (is_1 + is_2) + 2 * is_3

        def head_at(c, far):
            return 4 * c + (c * z + (1 - c) * y + far) % 4

        @pl.when(i == 0)
        def _():
            drain(anchor.at[pl.ds(0, 512)], r_core.at[0])

        @pl.when(i == 1)
        def _():
            pass_on(1)
            pass_on(2)

        @pl.when(i == 2)
        def _():
            pass_on(3)
            drain(anchor.at[pl.ds(0, 512)], r_core.at[1])
            drain(anchor.at[pl.ds(0, 512)], r_core.at[2])

        @pl.when(i == 3)
        def _():
            drain(anchor.at[pl.ds(0, 512)], r_core.at[3])

        @pl.when(i == MERGE_AT)
        def _():
            drain(part_in.at[pl.ds(0, 15 * 64)], r_part)
            drain(lse_in.at[pl.ds(0, 15)], r_lse)
            lse_all = lse_in[...]
            weight = jnp.exp2(lse_all - jnp.max(lse_all, axis=0, keepdims=True))
            weight = weight / jnp.sum(weight, axis=0, keepdims=True)
            merged = jnp.zeros((64, DH), f32)
            for j in range(16):
                column = jnp.sum(jnp.where(diag, weight[j, 0:1, :], 0.0), axis=1, keepdims=True)
                merged += column * part_in[j * 64:(j + 1) * 64, :].astype(f32)
            fin_out[...] = merged.reshape(8, 8, DH)

            def send_fin(d, carry):
                other = (member + d) % 8
                send(fin_out.at[other], fin_in.at[head], s_fin, r_fin, me - member + other)
                return carry

            lax.fori_loop(1, 8, send_fin, 0)
            fin_in[head] = fin_out[member]

        groups = (head_at(core_a, far_a), head_at(core_b, far_b))

        @pl.when(me != 0)
        def _():
            for g in groups:
                base = pl.multiple_of(g * 512, 512)
                keys = anchor[pl.ds(base, 256), :]
                values = jnp.concatenate([anchor[pl.ds(base + 256, 256), :], ones_first], axis=1)
                for h in range(GROUP):
                    cols = pl.ds(pl.multiple_of(g * GROUP * DH, GROUP * DH) + h * DH, DH)
                    s = lax.dot_general(q_ref[:, cols], keys, NT, preferred_element_type=f32)
                    lse = own_lse[:, cols]
                    peak = jnp.maximum(jnp.max(s, axis=1, keepdims=True) * EXP2_SCALE, lse)
                    p = jnp.concatenate(
                        [jnp.exp2(s[:, :DH] * EXP2_SCALE - peak), jnp.exp2(s[:, DH:] * EXP2_SCALE - peak)], axis=1).astype(bf16)
                    o = jnp.dot(p, values, preferred_element_type=f32)
                    scale = jnp.exp2(lse - peak)
                    mixed = (o[:, :DH] + scale * own_out[:, cols]) * pl.reciprocal(o[:, DH:] + scale, approx=True)
                    out_ref[:, cols] = mixed.astype(bf16)

        @pl.when(me == 0)
        def _():
            for g in groups:
                for h in range(GROUP):
                    cols = pl.ds(pl.multiple_of(g * GROUP * DH, GROUP * DH) + h * DH, DH)
                    out_ref[:, cols] = own_out[:, cols].astype(bf16)

        return carry

    lax.fori_loop(0, KVH // 2, anchor_block, 0)

    drain(fin_in.at[pl.ds(0, 7)], r_fin)
    answer_ref[...] = jnp.where(me < qlen_ref[0], fin_in[...].reshape(64, DH), 0.0)

    drain(rows_in.at[pl.ds(0, 7)], s_rows)
    drain(kvbuf.at[pl.ds(0, 7 * 512)], s_kv)
    drain(q_all.at[pl.ds(0, 15 * 64)], s_q)
    drain(part_in.at[pl.ds(0, 15 * 64)], s_part)
    drain(lse_in.at[pl.ds(0, 15)], s_lse)
    drain(fin_in.at[pl.ds(0, 7)], s_fin)
    drain(anchor.at[pl.ds(0, 3 * 128)], s_anc.at[2])
    for n in range(4):
        drain(anchor.at[pl.ds(0, 512)], s_core.at[n])
    for n in range(1, 4):
        drain(anchor.at[pl.ds(0, 512)], s_head.at[n])

    @pl.when(at[0] == 0)
    def _():
        drain(anchor.at[pl.ds(0, 3 * 128)], s_anc.at[1])

    @pl.when(me == 0)
    def _():
        drain(anchor.at[pl.ds(0, 2048)], s_anc.at[0])
        drain(anchor.at[pl.ds(0, 15 * 128)], s_anc.at[3])


def body(context_q, context_k, context_v, question, valid, qlen):
    hbm = pl.BlockSpec(memory_space=pltpu.HBM)
    vmem = pl.BlockSpec(memory_space=pltpu.VMEM)
    dma = pltpu.SemaphoreType.DMA
    encoded, answer = pl.pallas_call(
        star_kernel,
        out_shape=(jax.ShapeDtypeStruct((BLK, H * DH), bf16), jax.ShapeDtypeStruct((H, DH), f32)),
        in_specs=[hbm] * 5 + [pl.BlockSpec(memory_space=pltpu.SMEM)],
        out_specs=(vmem, vmem),
        scratch_shapes=[
            pltpu.VMEM((BLK, H * DH), bf16),
            pltpu.VMEM((BLK, KVH * DH), bf16),
            pltpu.VMEM((BLK, KVH * DH), bf16),
            pltpu.VMEM((1, H * DH), bf16),
            pltpu.SMEM((N,), jnp.int32),
            pltpu.VMEM((BLK, H * DH), f32),
            pltpu.VMEM((BLK, H * DH), f32),
            pltpu.VMEM((H, DH), f32),
            pltpu.VMEM((KVH * 512, DH), bf16),
            pltpu.VMEM((8 * 512, DH), bf16),
            pltpu.VMEM((8 * BLK, DH), bf16),
            pltpu.VMEM((8, 8, DH), f32),
            pltpu.VMEM((16 * 64, DH), bf16),
            pltpu.VMEM((16 * 64, DH), bf16),
            pltpu.VMEM((16, 8, DH), f32),
            pltpu.VMEM((16 * 64, DH), bf16),
            pltpu.VMEM((16, 8, DH), f32),
            pltpu.VMEM((8, 8, DH), f32),
            pltpu.VMEM((8, 8, DH), f32),
            pltpu.VMEM((KVH * 512, DH), bf16),
            dma((5,)), dma, dma, dma, dma((4,)), dma, dma, dma((4,)), dma((3,)), dma((4,)), dma((4,)), dma((4,)), dma((4,)), dma, dma, dma, dma, dma, dma, dma,
        ],
        compiler_params=pltpu.CompilerParams(collective_id=0, has_side_effects=True, vmem_limit_bytes=44 << 20),
        name="star",
    )(*[pltpu.with_memory_space_constraint(a, pltpu.HBM) for a in (context_q, context_k, context_v, question, valid)], qlen)
    return encoded, answer.reshape(1, H * DH).astype(bf16)


def solution(mesh):
    in_specs = (P("ctx", None), P("ctx", None), P("ctx", None), P("ctx", None), P(), P())
    out_specs = (P("ctx", None), P("ctx", None))
    return jax.shard_map(body, mesh=mesh, in_specs=in_specs, out_specs=out_specs, check_vma=False)
```

```python
import functools

import jax
import jax.numpy as jnp
from jax import lax
from jax.experimental import pallas as pl
from jax.experimental.pallas import tpu as pltpu
from jax.sharding import PartitionSpec as P

H = 64
KVH = 8
DH = 128
BLK = 256
N = 128
GROUP = H // KVH
EXP2_SCALE = 1.4426950408889634 * DH ** (-0.5)

f32 = jnp.float32
bf16 = jnp.bfloat16
MESH = pl.DeviceIdType.MESH
DEAD = 1e30
ORDER = (0, 1, 3, 2)
NT = (((1,), (1,)), ((), ()))

ROWS_AT = 1
SPREAD_AT = 1
GATHER_AT = 2
MERGE_AT = 2
GREETINGS = 9 + 1 + 15 + 7 + 7


def stride_of(axis):
    return 2 + 6 * axis + 9 * axis * (axis - 1)


def send(src, dst, send_sem, recv_sem, device):
    pltpu.make_async_remote_copy(
        src_ref=src, dst_ref=dst, send_sem=send_sem, recv_sem=recv_sem,
        device_id=(device,), device_id_type=MESH,
    ).start()


def drain(ref, sem):
    pltpu.make_async_copy(ref, ref, sem).wait()


def star_kernel(
    q_hbm, k_hbm, v_hbm, question_hbm, valid_hbm, qlen_ref,
    out_ref, answer_ref,
    q_ref, k_ref, v_ref, question_ref, valid_ref,
    own_out, own_lse, q64, kvs, kvbuf, ones, rows_in, q_all, part_out, lse_out, part_in, lse_in, fin_out, fin_in, anchor,
    load_sem, s_rows, r_rows, s_q, r_q, s_kv, r_kv, s_anc, r_anc, s_head, r_head, s_core, r_core, s_part, r_part, s_lse, r_lse, s_fin, r_fin, own_sem,
):
    me = lax.axis_index("ctx")
    core = me % 2
    x = (me // 2) % 4
    z = (me // 8) % 4
    y = me // 32
    cls = (x + y + z) % 4
    head = 2 * cls + core
    line = me // 8
    member = me % 8

    axis = head % 3
    stride = stride_of(axis)
    first = me - core - ((me // stride) % 4) * stride
    other_core = me + 1 - 2 * core

    st = (2 + 30 * core, 8 - 6 * core, 32 - 24 * core)
    at = [(me // step) % 4 for step in st]
    half = 2048 * core

    def along(n, d):
        return me + ((at[n] + d) % 4 - at[n]) * st[n]

    def peer_device(other):
        return (other * 4 + (cls + 8 - other // 4 - other % 4) % 4) * 2 + core

    def peer(d):
        other = (line + d) % 16
        return other, peer_device(other)

    barrier = pltpu.get_barrier_semaphore()

    def greet(device):
        pl.semaphore_signal(barrier, inc=1, device_id=(device,), device_id_type=MESH)

    @pl.when(jnp.logical_and(at[0] == 0, me != 0))
    def _():
        greet(0)

    for n in range(3):
        for d in (1, 2, 3):
            greet(along(n, d))
    greet(other_core)
    for d in range(1, 16):
        greet(peer(d)[1])
    for d in range(1, 8):
        greet(me - member + (member + d) % 8)
        source = ((me // stride) % 4 * 2 + core + d) % 8
        greet(first + source // 2 * stride + source % 2)

    loads = [
        pltpu.make_async_copy(src, dst, load_sem.at[n])
        for n, (src, dst) in enumerate([
            (valid_hbm, valid_ref), (k_hbm, k_ref), (v_hbm, v_ref), (question_hbm, question_ref),
            (q_hbm, q_ref)])
    ]
    for load in loads:
        load.start()

    for load in loads[:4]:
        load.wait()
    valid_here = valid_ref[me]
    row = lax.broadcasted_iota(jnp.int32, (BLK, DH), 0)
    live = row < valid_here
    for h in range(H):
        q64[h:h + 1, :] = question_ref[:, h * DH:(h + 1) * DH].astype(f32)
    for h in range(KVH):
        cols = slice(h * DH, (h + 1) * DH)
        k_h = k_ref[:, cols].astype(f32)
        v_h = v_ref[:, cols].astype(f32)
        kvs[h * 512:h * 512 + 256, :] = jnp.where(live, k_h, k_h[0:1, :]).astype(bf16)
        kvs[h * 512 + 256:h * 512 + 512, :] = jnp.where(live, v_h, 0.0).astype(bf16)
    @pl.when(me == 0)
    def _():
        pl.semaphore_wait(barrier, GREETINGS + 31)

    @pl.when(me != 0)
    def _():
        pl.semaphore_wait(barrier, GREETINGS)

    def send_rows(d, carry):
        other = (head + d) % 8
        target = me - member + ((other // 2 + 8 - y - z) % 4) * 2 + other % 2
        send(q64.at[pl.ds(other * 8, 8)], rows_in.at[member], s_rows, r_rows, target)
        return carry

    lax.fori_loop(1, 8, send_rows, 0)

    spread_rows = pl.ds(half + 512 * at[2] + 128 * at[1], 128)

    def send_spread():
        for d in (1, 2, 3):
            send(anchor.at[spread_rows], anchor.at[spread_rows], s_anc.at[1], r_anc.at[1], along(0, d))
        send_gather()

    def spread():
        @pl.when(jnp.logical_and(at[0] == 0, me != 0))
        def _():
            drain(anchor.at[pl.ds(0, 128)], r_anc.at[0])
            send_spread()

    def gather():
        @pl.when(at[0] != 0)
        def _():
            drain(anchor.at[pl.ds(0, 128)], r_anc.at[1])
            send_gather()

    def send_gather():
        for d in (1, 2, 3):
            send(anchor.at[spread_rows], anchor.at[spread_rows], s_anc.at[2], r_anc.at[2], along(1, d))

    def own_head(j):
        return 4 * core + (at[2] + ORDER[j]) % 4

    def share(j):
        rows = anchor.at[pl.ds(own_head(j) * 512, 512)]
        send(rows, rows, s_core.at[j], r_core.at[j], other_core)

    def gather_heads():
        drain(anchor.at[pl.ds(0, 3 * 128)], r_anc.at[2])
        share(0)
        rows = anchor.at[pl.ds(own_head(0) * 512, 512)]
        for j in (1, 2, 3):
            send(rows, rows, s_head.at[j], r_head.at[j], along(2, 4 - ORDER[j]))

    def pass_on(j):
        drain(anchor.at[pl.ds(0, 512)], r_head.at[j])
        share(j)

    @pl.when(me == 0)
    def _():
        def scatter(i, carry):
            j = ((i + 2) % 4) * 4 + (2 + 3 * (i // 4)) % 4
            piece = 2048 + 128 * ((j % 4) * 4 + j // 4)
            send(kvs.at[pl.ds(piece, 128)], anchor.at[pl.ds(piece, 128)], s_anc.at[0], r_anc.at[0], 8 * (j % 4) + 2 * (j // 4) + 1)

            @pl.when(j != 0)
            def _():
                piece = 128 * j
                send(kvs.at[pl.ds(piece, 128)], anchor.at[pl.ds(piece, 128)], s_anc.at[3], r_anc.at[0], 8 * j)

            return carry

        anchor[0:128, :] = kvs[0:128, :]
        lax.fori_loop(0, 16, scatter, 0)
        send_spread()

    def send_kv(d, carry):
        other = (head + d) % 8
        step = stride_of(other % 3)
        at = (me // step) % 4
        target = me - core + ((at + other // 2 + 4 - cls) % 4 - at) * step + other % 2
        send(kvs.at[pl.ds(other * 512, 512)], kvbuf.at[pl.ds((at * 2 + core) * 512, 512)], s_kv, r_kv, target)
        return carry

    at_home = (me // stride) % 4
    own_kv = pltpu.make_async_copy(
        kvs.at[pl.ds(head * 512, 512)], kvbuf.at[pl.ds((at_home * 2 + core) * 512, 512)], own_sem)
    own_kv.start()
    @pl.when(me > 1)
    def _():
        lax.fori_loop(1, 8, send_kv, 0)

    rows_in[member] = q64[pl.ds(head * 8, 8), :]
    for b in range(8):
        valid_b = valid_ref[first + (b // 2) * stride + b % 2]
        ones[b * BLK:(b + 1) * BLK, :] = jnp.where(row < valid_b, 1.0, 0.0).astype(bf16)

    loads[4].wait()
    causal = lax.broadcasted_iota(jnp.int32, (BLK, BLK), 1) <= lax.broadcasted_iota(jnp.int32, (BLK, BLK), 0)
    ones_own = jnp.where(live, 1.0, 0.0).astype(bf16)

    def own_block(n, carry):

        pl.when(n == SPREAD_AT)(spread)

        @pl.when(n == ROWS_AT)
        def _():
            drain(rows_in.at[pl.ds(0, 7)], r_rows)
            q_all[pl.ds(line * 64, 64), :] = rows_in[...].reshape(64, DH).astype(bf16)

            def send_q(d, carry):
                other, target = peer(d)
                send(q_all.at[pl.ds(line * 64, 64)], q_all.at[pl.ds(line * 64, 64)], s_q, r_q.at[y], target)
                return carry

            lax.fori_loop(1, 16, send_q, 0)


        @pl.when(n == 1)
        def _():
            @pl.when(me <= 1)
            def _():
                lax.fori_loop(1, 8, send_kv, 0)

        for g in (4 * n, 4 * n + 1, 4 * n + 2, 4 * n + 3):
            base = pl.multiple_of(g * 512, 512)
            keys = kvs[pl.ds(base, 256), :]
            values = jnp.concatenate([kvs[pl.ds(base + 256, 256), :], ones_own], axis=1)
            for h in range(GROUP):
                cols = pl.ds(pl.multiple_of(g * GROUP * DH, GROUP * DH) + h * DH, DH)
                s = lax.dot_general(q_ref[:, cols], keys, NT, preferred_element_type=f32)
                s = jnp.where(causal, s, -1e30)
                peak = jnp.max(s, axis=1, keepdims=True) * EXP2_SCALE
                p = jnp.exp2(s * EXP2_SCALE - peak).astype(bf16)
                o = jnp.dot(p, values, preferred_element_type=f32)
                own_out[:, cols] = jnp.where(live, o[:, :DH] * pl.reciprocal(o[:, DH:], approx=True), 0.0)
                own_lse[:, cols] = jnp.where(live, peak + jnp.log2(o[:, DH:]), DEAD)
        return carry

    lax.fori_loop(0, KVH // 4, own_block, 0)

    gather()

    own_kv.wait()
    drain(kvbuf.at[pl.ds(0, 7 * 512)], r_kv)

    diag = lax.broadcasted_iota(jnp.int32, (64, DH), 0) == lax.broadcasted_iota(jnp.int32, (64, DH), 1)

    def attend(i, carry):
        pl.when(i == GATHER_AT)(gather_heads)
        chunk = (i + y) % 4

        @pl.when(i == 0)
        def _():
            drain(q_all.at[pl.ds(0, 3 * 64)], r_q.at[chunk])

        @pl.when(i != 0)
        def _():
            drain(q_all.at[pl.ds(0, 4 * 64)], r_q.at[chunk])

        rows = pl.ds(pl.multiple_of(chunk * 256, 256), 256)
        q = q_all[rows, :]
        peak = None
        for b in range(0, 8, 2):
            keys = jnp.concatenate([kvbuf[n * 512:n * 512 + 256, :] for n in (b, b + 1)], axis=0)
            values = jnp.concatenate(
                [jnp.concatenate([kvbuf[n * 512 + 256:n * 512 + 512, :], ones[n * BLK:(n + 1) * BLK, :]], axis=1) for n in (b, b + 1)],
                axis=0)
            s = lax.dot_general(q, keys, NT, preferred_element_type=f32)
            new_peak = jnp.max(s, axis=1, keepdims=True) * EXP2_SCALE
            if peak is not None:
                new_peak = jnp.maximum(peak, new_peak)
            p = jnp.exp2(s * EXP2_SCALE - new_peak).astype(bf16)
            o_b = jnp.dot(p, values, preferred_element_type=f32)
            o = o_b if peak is None else o * jnp.exp2(peak - new_peak) + o_b
            peak = new_peak
        total = o[:, DH:]
        part_out[rows, :] = (o[:, :DH] * pl.reciprocal(total, approx=True)).astype(bf16)
        lse = peak + jnp.log2(total)
        for n in range(4):
            other = 4 * chunk + n
            flat = jnp.sum(jnp.where(diag, lse[n * 64:(n + 1) * 64], 0.0), axis=0, keepdims=True)
            lse_out[other] = jnp.broadcast_to(flat, (8, DH))

            @pl.when(other != line)
            def _():
                target = peer_device(other)
                send(part_out.at[pl.ds(other * 64, 64)], part_in.at[pl.ds(line * 64, 64)], s_part, r_part, target)
                send(lse_out.at[other], lse_in.at[line], s_lse, r_lse, target)
        return carry

    lax.fori_loop(0, 4, attend, 0)
    part_in[pl.ds(line * 64, 64), :] = part_out[pl.ds(line * 64, 64), :]
    lse_in[line] = lse_out[line]

    ones_first = jnp.where(row < valid_ref[0], 1.0, 0.0).astype(bf16)

    def anchor_block(i, carry):
        is_1, is_2, is_3 = i * (2 - i) * (3 - i) // 2, i * (i - 1) * (3 - i) // 2, i * (i - 1) * (i - 2) // 6
        core_a, core_b = (core + is_2) % 2, (core + 1 - is_1) % 2
        far_a, far_b = is_1 + is_2 + 2 * is_3, 3 * (is_1 + is_2) + 2 * is_3

        def head_at(c, far):
            return 4 * c + (c * z + (1 - c) * y + far) % 4

        @pl.when(i == 0)
        def _():
            drain(anchor.at[pl.ds(0, 512)], r_core.at[0])

        @pl.when(i == 1)
        def _():
            pass_on(1)
            pass_on(2)

        @pl.when(i == 2)
        def _():
            pass_on(3)
            drain(anchor.at[pl.ds(0, 512)], r_core.at[1])
            drain(anchor.at[pl.ds(0, 512)], r_core.at[2])

        @pl.when(i == 3)
        def _():
            drain(anchor.at[pl.ds(0, 512)], r_core.at[3])

        @pl.when(i == MERGE_AT)
        def _():
            drain(part_in.at[pl.ds(0, 15 * 64)], r_part)
            drain(lse_in.at[pl.ds(0, 15)], r_lse)
            lse_all = lse_in[...]
            weight = jnp.exp2(lse_all - jnp.max(lse_all, axis=0, keepdims=True))
            weight = weight / jnp.sum(weight, axis=0, keepdims=True)
            merged = jnp.zeros((64, DH), f32)
            for j in range(16):
                column = jnp.sum(jnp.where(diag, weight[j, 0:1, :], 0.0), axis=1, keepdims=True)
                merged += column * part_in[j * 64:(j + 1) * 64, :].astype(f32)
            fin_out[...] = merged.reshape(8, 8, DH)

            def send_fin(d, carry):
                other = (member + d) % 8
                send(fin_out.at[other], fin_in.at[head], s_fin, r_fin, me - member + other)
                return carry

            lax.fori_loop(1, 8, send_fin, 0)
            fin_in[head] = fin_out[member]

        groups = (head_at(core_a, far_a), head_at(core_b, far_b))

        @pl.when(me != 0)
        def _():
            for g in groups:
                base = pl.multiple_of(g * 512, 512)
                keys = anchor[pl.ds(base, 256), :]
                values = jnp.concatenate([anchor[pl.ds(base + 256, 256), :], ones_first], axis=1)
                for h in range(GROUP):
                    cols = pl.ds(pl.multiple_of(g * GROUP * DH, GROUP * DH) + h * DH, DH)
                    s = lax.dot_general(q_ref[:, cols], keys, NT, preferred_element_type=f32)
                    lse = own_lse[:, cols]
                    peak = jnp.maximum(jnp.max(s, axis=1, keepdims=True) * EXP2_SCALE, lse)
                    p = jnp.concatenate(
                        [jnp.exp2(s[:, :DH] * EXP2_SCALE - peak), jnp.exp2(s[:, DH:] * EXP2_SCALE - peak)], axis=1).astype(bf16)
                    o = jnp.dot(p, values, preferred_element_type=f32)
                    scale = jnp.exp2(lse - peak)
                    mixed = (o[:, :DH] + scale * own_out[:, cols]) * pl.reciprocal(o[:, DH:] + scale, approx=True)
                    out_ref[:, cols] = mixed.astype(bf16)

        @pl.when(me == 0)
        def _():
            for g in groups:
                for h in range(GROUP):
                    cols = pl.ds(pl.multiple_of(g * GROUP * DH, GROUP * DH) + h * DH, DH)
                    out_ref[:, cols] = own_out[:, cols].astype(bf16)

        return carry

    lax.fori_loop(0, KVH // 2, anchor_block, 0)

    drain(fin_in.at[pl.ds(0, 7)], r_fin)
    answer_ref[...] = jnp.where(me < qlen_ref[0], fin_in[...].reshape(64, DH), 0.0)

    drain(rows_in.at[pl.ds(0, 7)], s_rows)
    drain(kvbuf.at[pl.ds(0, 7 * 512)], s_kv)
    drain(q_all.at[pl.ds(0, 15 * 64)], s_q)
    drain(part_in.at[pl.ds(0, 15 * 64)], s_part)
    drain(lse_in.at[pl.ds(0, 15)], s_lse)
    drain(fin_in.at[pl.ds(0, 7)], s_fin)
    drain(anchor.at[pl.ds(0, 3 * 128)], s_anc.at[2])
    for n in range(4):
        drain(anchor.at[pl.ds(0, 512)], s_core.at[n])
    for n in range(1, 4):
        drain(anchor.at[pl.ds(0, 512)], s_head.at[n])

    @pl.when(at[0] == 0)
    def _():
        drain(anchor.at[pl.ds(0, 3 * 128)], s_anc.at[1])

    @pl.when(me == 0)
    def _():
        drain(anchor.at[pl.ds(0, 2048)], s_anc.at[0])
        drain(anchor.at[pl.ds(0, 15 * 128)], s_anc.at[3])


def body(context_q, context_k, context_v, question, valid, qlen):
    hbm = pl.BlockSpec(memory_space=pltpu.HBM)
    vmem = pl.BlockSpec(memory_space=pltpu.VMEM)
    dma = pltpu.SemaphoreType.DMA
    encoded, answer = pl.pallas_call(
        star_kernel,
        out_shape=(jax.ShapeDtypeStruct((BLK, H * DH), bf16), jax.ShapeDtypeStruct((H, DH), f32)),
        in_specs=[hbm] * 5 + [pl.BlockSpec(memory_space=pltpu.SMEM)],
        out_specs=(vmem, vmem),
        scratch_shapes=[
            pltpu.VMEM((BLK, H * DH), bf16),
            pltpu.VMEM((BLK, KVH * DH), bf16),
            pltpu.VMEM((BLK, KVH * DH), bf16),
            pltpu.VMEM((1, H * DH), bf16),
            pltpu.SMEM((N,), jnp.int32),
            pltpu.VMEM((BLK, H * DH), f32),
            pltpu.VMEM((BLK, H * DH), f32),
            pltpu.VMEM((H, DH), f32),
            pltpu.VMEM((KVH * 512, DH), bf16),
            pltpu.VMEM((8 * 512, DH), bf16),
            pltpu.VMEM((8 * BLK, DH), bf16),
            pltpu.VMEM((8, 8, DH), f32),
            pltpu.VMEM((16 * 64, DH), bf16),
            pltpu.VMEM((16 * 64, DH), bf16),
            pltpu.VMEM((16, 8, DH), f32),
            pltpu.VMEM((16 * 64, DH), bf16),
            pltpu.VMEM((16, 8, DH), f32),
            pltpu.VMEM((8, 8, DH), f32),
            pltpu.VMEM((8, 8, DH), f32),
            pltpu.VMEM((KVH * 512, DH), bf16),
            dma((5,)), dma, dma, dma, dma((4,)), dma, dma, dma((4,)), dma((3,)), dma((4,)), dma((4,)), dma((4,)), dma((4,)), dma, dma, dma, dma, dma, dma, dma,
        ],
        compiler_params=pltpu.CompilerParams(collective_id=0, has_side_effects=True, vmem_limit_bytes=44 << 20),
        name="star",
    )(*[pltpu.with_memory_space_constraint(a, pltpu.HBM) for a in (context_q, context_k, context_v, question, valid)], qlen)
    return encoded, answer.reshape(1, H * DH).astype(bf16)


def solution(mesh):
    in_specs = (P("ctx", None), P("ctx", None), P("ctx", None), P("ctx", None), P(), P())
    out_specs = (P("ctx", None), P("ctx", None))
    return jax.shard_map(body, mesh=mesh, in_specs=in_specs, out_specs=out_specs, check_vma=False)
```
